256 devices in a mesh: seq: 128 (over z, y, x), grp: 2 (over core).
Axes of the slice: x: 4, y: 4, z: 8, core: 2. Of those that a mesh axis runs over, the one named last changes fastest.
Arguments:
- queries: bfloat16 [65536, 3072], P('seq', 'grp'), parts along dimension 1, may hold values from -124 to 124
- keys: bfloat16 [65536, 384], P('seq', 'grp'), parts along dimension 1, may hold values from -4.2 to 4.2
- values: bfloat16 [65536, 256], P('seq', 'grp'), parts along dimension 1, may hold values from -6 to 6
- selected: int32 [1024, 32], P('seq', 'grp'), parts along dimension 1, may hold values from 0 to 1023, as said below
- d_out: bfloat16 [65536, 2048], P('seq', 'grp'), parts along dimension 1, may hold values from -6 to 6
Outputs:
- attended: bfloat16 [65536, 2048], P('seq', 'grp'), parts along dimension 1
- d_queries: bfloat16 [65536, 3072], P('seq', 'grp'), parts along dimension 1
- d_keys: bfloat16 [65536, 384], P('seq', 'grp'), parts along dimension 1
- d_values: bfloat16 [65536, 256], P('seq', 'grp'), parts along dimension 1
The draws below stay inside these ranges and needn't reach their ends.
There are 2 independent parts, one for each index of `grp`. The reference program is written for one: setup_inputs(seed, part) draws one part's arguments, and reference() takes and returns one part's arrays. A program takes and returns all parts, laid end to end along the dimension named above; each array names one. Nothing has to cross between parts.
Inputs may be any that keep to these rules, and one draw needn't show every extreme that they name: `selected`: entry 0 of each list is the query block itself; every other entry names a block that ends before the query block starts, or repeats the query block itself. Over the 8 rows of one device, the entries that lie on any one other device name at most one distinct block, and some other device is named. Over the rows of one device, no other device is named by more than 1 entries, and in every draw some device's rows name some other device exactly 1 times.
All inputs are finite; a program needn't handle non-finite values.
Results may differ from the reference program's by a relative error of at most 0.03.
Values may be sent and summed in bfloat16 or wider, within the bound.
No kernel may reach another device: no remote copies, remote signals or barrier semaphores. Data moves between devices by JAX's collectives and lax.ppermute only.
A program may use at most 128 MiB of HBM per device.

```python
import jax
import jax.numpy as jnp
from jax import lax

HEADS = 8
DK = 192
DV = 128
BLK = 64
SEL = 16
TOK_DEV = 512
HALF = 256
TOKENS = 65536
QBLOCKS = 1024
N_SEQ = 128


def draw_keys(key, part):
    key = jax.random.fold_in(key, 3)
    return jnp.clip(jax.random.normal(key, (TOKENS, DK), jnp.float32), -4.0, 4.0).astype(jnp.bfloat16)


def draw_queries(key, part):
    key = jax.random.fold_in(key, 5)
    return jnp.clip(jax.random.normal(key, (TOKENS, HEADS * DK), jnp.float32), -4.0, 4.0).astype(jnp.bfloat16)


def draw_selected(key, part):
    key = jax.random.fold_in(key, 11)
    pick_key, order_key = jax.random.split(key)
    local_blocks = TOK_DEV // BLK
    per_half = local_blocks // 2
    devices = jnp.arange(N_SEQ, dtype=jnp.int32)
    within = jax.random.randint(pick_key, (N_SEQ, N_SEQ), 0, per_half)
    candidate = (devices[None, :] * per_half + within).astype(jnp.int32)
    ranking = jax.random.randint(order_key, (N_SEQ, N_SEQ), 0, 1 << 20) * N_SEQ + devices[None, :]
    ordering = jnp.argsort(ranking, axis=1).astype(jnp.int32)
    block_ids = jnp.arange(local_blocks, dtype=jnp.int32)
    is_late = block_ids >= per_half
    half_index = jnp.where(is_late[None, :], 2 * N_SEQ - 1 - devices[:, None], devices[:, None])
    own_block = (half_index * per_half + block_ids[None, :] % per_half).astype(jnp.int32)
    slot_ids = jnp.arange(1, SEL, dtype=jnp.int32)
    turn = (block_ids[:, None] * (SEL - 1) + slot_ids[None, :] - 1) % N_SEQ
    owners = ordering[:, turn]
    picked = candidate[devices[:, None, None], owners]
    allowed = is_late[None, :, None] | (owners < devices[:, None, None])
    entries = jnp.where(allowed, picked, own_block[:, :, None])
    lists = jnp.concatenate([own_block[:, :, None], entries], axis=2)
    return lists.reshape(N_SEQ * local_blocks, SEL).astype(jnp.int32)


def level_of(rng, extent, shards, least, top_value):
    factor_of, own = 1.0, jax.random.fold_in(rng, 6)
    for dim, shards_of in shards:
        steps = jnp.exp(jax.random.uniform(jax.random.fold_in(own, dim), (shards_of,), jnp.float32, least / len(shards), top_value / len(shards)))
        factor_of = factor_of * jnp.repeat(steps, extent[dim] // shards_of).reshape([-1 if axis == dim else 1 for axis in range(len(extent))])
    return factor_of


def bell_draw(stream_key, extent, width, bound, cuts=(), held_as=jnp.bfloat16):
    values = jax.random.normal(stream_key, extent, jnp.float32) * width
    if len(cuts) > 0:
        values = level_of(stream_key, extent, cuts, -0.22, 0.18) * values
    return jnp.clip(values, min=-bound, max=bound).astype(held_as)


def setup_inputs(seed: int = 0, part: int = 0) -> dict:
    splits = jax.random.split(jax.random.key(seed), 6)
    own_keys = jax.random.split(jax.random.fold_in(splits[5], part), 6)
    return {
        "queries": draw_queries(jax.random.fold_in(jax.random.fold_in(splits[5], part), 71), part),
        "keys": draw_keys(jax.random.fold_in(jax.random.fold_in(splits[5], part), 71), part),
        "values": bell_draw(own_keys[2], (TOKENS, DV), 1.0, 6.0, ((0, 128),)),
        "selected": draw_selected(jax.random.fold_in(jax.random.fold_in(splits[5], part), 71), part),
        "d_out": bell_draw(own_keys[4], (TOKENS, HEADS * DV), 1.0, 6.0, ((0, 128),)),
    }


def block_grads(q_rows, k_rows, v_rows, do_rows, q_pos, k_pos):
    width_k = k_rows.shape[1]
    width_v = v_rows.shape[1]
    head_count = q_rows.shape[1] // width_k
    block_len = q_rows.shape[0]
    score_scale = width_k ** -0.5
    query_mat = q_rows.reshape(block_len, head_count, width_k).transpose(1, 0, 2).reshape(head_count * block_len, width_k)
    grad_mat = do_rows.reshape(block_len, head_count, width_v).transpose(1, 0, 2).reshape(head_count * block_len, width_v)
    visible = jnp.tile(k_pos[None, :] <= q_pos[:, None], (head_count, 1))
    scores = lax.dot_general(query_mat, k_rows, (((1,), (1,)), ((), ())), preferred_element_type=jnp.float32) * score_scale
    scores = jnp.where(visible, scores, -jnp.inf)
    row_max = jnp.max(scores, axis=1, keepdims=True)
    expons = jnp.exp(scores - row_max)
    probs = expons / jnp.sum(expons, axis=1, keepdims=True)
    probs_low = probs.astype(jnp.bfloat16)
    attended = jnp.dot(probs_low, v_rows, preferred_element_type=jnp.float32).astype(jnp.bfloat16)
    d_probs = lax.dot_general(grad_mat, v_rows, (((1,), (1,)), ((), ())), preferred_element_type=jnp.float32)
    row_delta = jnp.sum(grad_mat.astype(jnp.float32) * attended.astype(jnp.float32), axis=1, keepdims=True)
    d_scores = (probs * (d_probs - row_delta)).astype(jnp.bfloat16)
    d_query = (jnp.dot(d_scores, k_rows, preferred_element_type=jnp.float32) * score_scale).astype(jnp.bfloat16)
    d_key = lax.dot_general(d_scores, query_mat, (((0,), (0,)), ((), ())), preferred_element_type=jnp.float32) * score_scale
    d_value = lax.dot_general(probs_low, grad_mat, (((0,), (0,)), ((), ())), preferred_element_type=jnp.float32)
    attended = attended.reshape(head_count, block_len, width_v).transpose(1, 0, 2).reshape(block_len, head_count * width_v)
    d_query = d_query.reshape(head_count, block_len, width_k).transpose(1, 0, 2).reshape(block_len, head_count * width_k)
    return attended, d_query, d_key, d_value


def stored_row(position):
    half_index = position // HALF
    is_late = half_index >= N_SEQ
    owners = jnp.where(is_late, 2 * N_SEQ - 1 - half_index, half_index)
    inner_pos = position % HALF + jnp.where(is_late, HALF, 0)
    return (owners * TOK_DEV + inner_pos).astype(jnp.int32)


def row_position(row_ids):
    owners = row_ids // TOK_DEV
    inner_pos = row_ids % TOK_DEV
    early = owners * HALF + inner_pos
    late = (2 * N_SEQ - 1 - owners) * HALF + inner_pos - HALF
    return jnp.where(inner_pos < HALF, early, late).astype(jnp.int32)


def reference(queries, keys, values, selected, d_out):
    offsets = jnp.arange(BLK, dtype=jnp.int32)

    def visit_block(carry, block_index):
        acc_key, acc_value = carry
        row_ids = (block_index * BLK + offsets).astype(jnp.int32)
        q_pos = row_position(row_ids)
        k_pos = (selected[block_index][:, None] * BLK + offsets[None, :]).reshape(-1).astype(jnp.int32)
        key_rows = stored_row(k_pos)
        attended, d_query, d_key, d_value = block_grads(queries[row_ids], keys[key_rows], values[key_rows], d_out[row_ids], q_pos, k_pos)
        return (acc_key.at[key_rows].add(d_key), acc_value.at[key_rows].add(d_value)), (attended, d_query)

    zero_grads = (jnp.zeros((TOKENS, DK), jnp.float32), jnp.zeros((TOKENS, DV), jnp.float32))
    (acc_key, acc_value), (attended, d_query) = lax.scan(visit_block, zero_grads, jnp.arange(QBLOCKS, dtype=jnp.int32))
    return (attended.reshape(TOKENS, HEADS * DV), d_query.reshape(TOKENS, HEADS * DK),
            acc_key.astype(jnp.bfloat16), acc_value.astype(jnp.bfloat16))
```

```python
import functools

import jax
import jax.numpy as jnp
from jax import lax
from jax.experimental import pallas as pl
from jax.experimental.pallas import tpu as pltpu
from jax.sharding import Mesh, PartitionSpec as P

BLK = 64
SEL = 16
HEADS = 8
DK = 192
DV = 128
ROWS = 160
SIDES = (8, 4, 4)
LOCAL = 8
CHUNK = 256
LOG2E = 1.4426950408889634
NEG = -1e30
BF = jnp.bfloat16
F32 = jnp.float32


def params(mib=56):
    return pltpu.CompilerParams(vmem_limit_bytes=mib * 1024 * 1024)


def pack_kernel(k_ref, v_ref, out_ref):
    for b in range(LOCAL):
        rows = slice(b * BLK, (b + 1) * BLK)
        k = k_ref[rows, :]
        out_ref[b, 0:BLK] = v_ref[rows, :]
        out_ref[b, BLK : 2 * BLK] = k[:, :128]
        low = k[:, 128:]
        out_ref[b, 2 * BLK :] = jnp.concatenate([low[:32], low[32:]], axis=1)


def pack(keys, values):
    return pl.pallas_call(
        pack_kernel,
        out_shape=jax.ShapeDtypeStruct((LOCAL, ROWS, 128), BF),
        compiler_params=params(),
        name="pack",
    )(keys, values)


def build_kernel(req_ref, table_ref, out_ref):
    c = pl.program_id(0)
    for z in range(table_ref.shape[0]):
        r = req_ref[c, z]

        @pl.when(r > 0)
        def _():
            out_ref[0, z] = table_ref[z, r - 1]


def build(req, table, plane):
    depth = table.shape[0]
    return pl.pallas_call(
        build_kernel,
        grid_spec=pltpu.PrefetchScalarGridSpec(
            num_scalar_prefetch=1,
            grid=(plane,),
            in_specs=[pl.BlockSpec((depth, LOCAL, ROWS, 128), lambda c, req: (0, 0, 0, 0))],
            out_specs=pl.BlockSpec((1, depth, ROWS, 128), lambda c, req: (c, 0, 0, 0)),
        ),
        out_shape=jax.ShapeDtypeStruct((plane, depth, ROWS, 128), BF),
        compiler_params=params(),
        name="build",
    )(req, table)


def sum_kernel(req_ref, ret_ref, out_ref, acc_ref):
    z = pl.program_id(0)
    acc_ref[...] = jnp.zeros_like(acc_ref)
    for c in range(ret_ref.shape[0]):
        r = req_ref[c, z]

        @pl.when(r > 0)
        def _():
            acc_ref[r - 1] += ret_ref[c, 0].astype(F32)

    out_ref[0] = acc_ref[...].astype(BF)


def sum_returned(req, returned):
    plane, depth = returned.shape[:2]
    return pl.pallas_call(
        sum_kernel,
        grid_spec=pltpu.PrefetchScalarGridSpec(
            num_scalar_prefetch=1,
            grid=(depth,),
            in_specs=[pl.BlockSpec((plane, 1, ROWS, 128), lambda z, req: (0, z, 0, 0))],
            out_specs=pl.BlockSpec((1, LOCAL, ROWS, 128), lambda z, req: (z, 0, 0, 0)),
            scratch_shapes=[pltpu.VMEM((LOCAL, ROWS, 128), F32)],
        ),
        out_shape=jax.ShapeDtypeStruct((depth, LOCAL, ROWS, 128), BF),
        compiler_params=params(),
        name="sum_returned",
    )(req, returned)


def finish_kernel(own_ref, got_ref, dk_ref, dv_ref):
    for b in range(LOCAL):
        rows = slice(b * BLK, (b + 1) * BLK)
        total = own_ref[b] + got_ref[b].astype(F32)
        dv_ref[rows, :] = total[0:BLK].astype(BF)
        low = total[2 * BLK :]
        low = jnp.concatenate([low[:, :64], low[:, 64:]], axis=0)
        dk_ref[rows, :] = jnp.concatenate([total[BLK : 2 * BLK], low], axis=1).astype(BF)


def finish(own, got):
    return pl.pallas_call(
        finish_kernel,
        out_shape=(
            jax.ShapeDtypeStruct((LOCAL * BLK, DK), BF),
            jax.ShapeDtypeStruct((LOCAL * BLK, DV), BF),
        ),
        compiler_params=params(),
        name="finish",
    )(own, got)


def dot(a, b, da, db):
    return lax.dot_general(a, b, (((da,), (db,)), ((), ())), preferred_element_type=F32)


def attend_kernel(
    src_ref,
    q_ref,
    do_ref,
    local_ref,
    got_ref,
    att_ref,
    dq_ref,
    part_ref,
    own_ref,
    k_buf,
    v_buf,
    q_buf,
    do_buf,
    p_buf,
    pb_buf,
):
    b = pl.program_id(0)
    depth = got_ref.shape[1]
    scale = DK**-0.5
    queries = HEADS * BLK

    @pl.when(b == 0)
    def _():
        own_ref[...] = jnp.zeros_like(own_ref)
        v_buf[:, 128:] = jnp.ones((SEL * BLK, 128), BF)
        row = lax.broadcasted_iota(jnp.int32, (BLK, BLK), 0)
        col = lax.broadcasted_iota(jnp.int32, (BLK, BLK), 1)
        one_hot = (row == col).astype(BF)
        for h in range(HEADS):
            q_buf[h * BLK : (h + 1) * BLK, DK:] = one_hot

    def place(e, tile, hidden):
        rows = slice(e * BLK, (e + 1) * BLK)
        v_buf[rows, 0:128] = tile[0:BLK]
        k_buf[rows, 0:128] = tile[BLK : 2 * BLK]
        low = tile[2 * BLK :]
        low = jnp.concatenate([low[:, :64], low[:, 64:]], axis=0)
        k_buf[rows, 128:] = jnp.concatenate([low, hidden], axis=1)

    nothing = jnp.zeros((BLK, BLK), BF)
    key_id = lax.broadcasted_iota(jnp.int32, (BLK, BLK), 0)
    query_id = lax.broadcasted_iota(jnp.int32, (BLK, BLK), 1)
    later = jnp.where(key_id > query_id, NEG, 0.0).astype(BF)
    for e in range(SEL):
        s = src_ref[b, e]

        @pl.when(s >= 0)
        def _():
            place(e, got_ref[s // depth, s % depth], nothing)

        @pl.when(s < 0)
        def _():
            place(e, local_ref[-1 - s], jnp.where(-1 - s == b, later, nothing))

    for h in range(HEADS):
        q_buf[h * BLK : (h + 1) * BLK, 0:DK] = q_ref[:, h * DK : (h + 1) * DK]

    q_all = q_buf[...]
    top = None
    for i in range(0, SEL * BLK, CHUNK):
        s = dot(k_buf[i : i + CHUNK, :], q_all, 1, 1)
        p_buf[i : i + CHUNK, :] = s
        m = jnp.max(s, axis=0, keepdims=True)
        top = m if top is None else jnp.maximum(top, m)
    out_t = None
    for i in range(0, SEL * BLK, CHUNK):
        p = jnp.exp2((p_buf[i : i + CHUNK, :] - top) * (scale * LOG2E))
        p_buf[i : i + CHUNK, :] = p
        pb = p.astype(BF)
        pb_buf[i : i + CHUNK, :] = pb
        o = dot(v_buf[i : i + CHUNK, :], pb, 0, 0)
        out_t = o if out_t is None else out_t + o
    out = jnp.transpose(out_t)
    inverse = 1.0 / out[:, 128:129]
    att = (out[:, :128] * inverse).astype(BF)
    for h in range(HEADS):
        rows = slice(h * BLK, (h + 1) * BLK)
        att_ref[:, h * DV : (h + 1) * DV] = att[rows]
        do = (do_ref[:, h * DV : (h + 1) * DV].astype(F32) * inverse[rows]).astype(BF)
        delta = jnp.sum(do.astype(F32) * att[rows].astype(F32), axis=1, keepdims=True)
        high = delta.astype(BF)
        rest = delta - high.astype(F32)
        mid = rest.astype(BF)
        last = (rest - mid.astype(F32)).astype(BF)
        lane = lax.broadcasted_iota(jnp.int32, (BLK, 128), 1)
        extra = jnp.where(
            lane == 0,
            high.astype(F32),
            jnp.where(lane == 1, mid.astype(F32), jnp.where(lane == 2, last.astype(F32), 0.0)),
        )
        do_buf[rows, 0:128] = do
        do_buf[rows, 128:] = (-extra).astype(BF)
    do_all = do_buf[...]
    dq_t = None
    for i in range(0, SEL * BLK, CHUNK):
        dp = dot(v_buf[i : i + CHUNK, :], do_all, 1, 1)
        ds = (p_buf[i : i + CHUNK, :] * dp).astype(BF)
        dv = dot(pb_buf[i : i + CHUNK, :], do_buf[:, 0:128], 1, 0)
        dk = dot(ds, q_all, 1, 0) * scale
        g = dot(k_buf[i : i + CHUNK, :], ds, 0, 0)
        dq_t = g if dq_t is None else dq_t + g
        for j in range(CHUNK // BLK):
            e = i // BLK + j
            rows = slice(j * BLK, (j + 1) * BLK)
            low = dk[rows, 128:DK]
            low = jnp.concatenate([low[:32], low[32:]], axis=1)
            tile = jnp.concatenate([dv[rows], dk[rows, :128], low], axis=0)
            s = src_ref[b, e]

            @pl.when(s >= 0)
            def _():
                part_ref[s // depth, s % depth] = tile.astype(BF)

            @pl.when(s < 0)
            def _():
                own_ref[-1 - s] += tile
    dq = (jnp.transpose(dq_t[:DK]) * scale).astype(BF)
    for h in range(0, HEADS, 2):
        dq_ref[:, h * DK : (h + 2) * DK] = jnp.concatenate(
            [dq[h * BLK : (h + 1) * BLK], dq[(h + 1) * BLK : (h + 2) * BLK]], axis=1
        )


def attend(src, queries, d_out, local, got):
    plane, depth = got.shape[:2]
    tokens = LOCAL * BLK
    keys = SEL * BLK
    rows = HEADS * BLK
    whole = pl.BlockSpec(got.shape, lambda b, src: (0, 0, 0, 0))
    return pl.pallas_call(
        attend_kernel,
        grid_spec=pltpu.PrefetchScalarGridSpec(
            num_scalar_prefetch=1,
            grid=(LOCAL,),
            in_specs=[
                pl.BlockSpec((BLK, HEADS * DK), lambda b, src: (b, 0)),
                pl.BlockSpec((BLK, HEADS * DV), lambda b, src: (b, 0)),
                pl.BlockSpec((LOCAL, ROWS, 128), lambda b, src: (0, 0, 0)),
                whole,
            ],
            out_specs=[
                pl.BlockSpec((BLK, HEADS * DV), lambda b, src: (b, 0)),
                pl.BlockSpec((BLK, HEADS * DK), lambda b, src: (b, 0)),
                whole,
                pl.BlockSpec((LOCAL, ROWS, 128), lambda b, src: (0, 0, 0)),
            ],
            scratch_shapes=[
                pltpu.VMEM((keys, 256), BF),
                pltpu.VMEM((keys, 256), BF),
                pltpu.VMEM((rows, 256), BF),
                pltpu.VMEM((rows, 256), BF),
                pltpu.VMEM((keys, rows), F32),
                pltpu.VMEM((keys, rows), BF),
            ],
        ),
        out_shape=(
            jax.ShapeDtypeStruct((tokens, HEADS * DV), BF),
            jax.ShapeDtypeStruct((tokens, HEADS * DK), BF),
            jax.ShapeDtypeStruct(got.shape, BF),
            jax.ShapeDtypeStruct((LOCAL, ROWS, 128), F32),
        ),
        compiler_params=params(),
        name="attend",
    )(src, queries, d_out, local, got)


def shards(depth, plane, queries, keys, values, selected, d_out):
    me = lax.axis_index(("z", "y", "x"))
    seq_count = depth * plane
    per_half = LOCAL // 2
    half_index = selected // per_half
    is_late = half_index >= seq_count
    owners = jnp.where(is_late, 2 * seq_count - 1 - half_index, half_index)
    inner = selected % per_half + jnp.where(is_late, per_half, 0)
    remote = owners != me
    slots = (owners % plane) * depth + owners // plane
    src = jnp.where(remote, slots, -1 - inner).astype(jnp.int32)
    flat = src.reshape(-1)
    hits = flat[:, None] == jnp.arange(seq_count, dtype=jnp.int32)[None, :]
    wanted = jnp.max(jnp.where(hits, inner.reshape(-1)[:, None] + 1, 0), axis=0)
    asked = lax.all_to_all(
        wanted.reshape(plane, 1, depth), ("y", "x"), split_axis=0, concat_axis=0, tiled=True
    ).reshape(plane, depth)
    local = pack(keys, values)
    table = lax.all_gather(local, "z")
    outgoing = build(asked, table, plane)
    got = lax.all_to_all(outgoing, ("y", "x"), split_axis=0, concat_axis=0, tiled=True)
    attended, d_queries, partial, own = attend(src, queries, d_out, local, got)
    returned = lax.all_to_all(partial, ("y", "x"), split_axis=0, concat_axis=0, tiled=True)
    sums = sum_returned(asked, returned)
    mine = lax.psum_scatter(sums, "z", scatter_dimension=0)
    d_keys, d_values = finish(own, mine)
    return attended, d_queries, d_keys, d_values


def solution(mesh):
    grid = Mesh(mesh.devices.reshape(SIDES + (-1,)), ("z", "y", "x", "grp"))
    spec = P(("z", "y", "x"), "grp")
    return jax.shard_map(
        functools.partial(shards, SIDES[0], SIDES[1] * SIDES[2]),
        mesh=grid,
        in_specs=(spec,) * 5,
        out_specs=(spec,) * 4,
        check_vma=False,
    )
```

```python
import functools

import jax
import jax.numpy as jnp
from jax import lax
from jax.experimental import pallas as pl
from jax.experimental.pallas import tpu as pltpu
from jax.sharding import Mesh, PartitionSpec as P

BLK = 64
SEL = 16
HEADS = 8
DK = 192
DV = 128
ROWS = 160
SIDES = (8, 4, 4)
LOCAL = 8
LOG2E = 1.4426950408889634
NEG = -1e30
BF = jnp.bfloat16
F32 = jnp.float32


def params(mib=56):
    return pltpu.CompilerParams(vmem_limit_bytes=mib * 1024 * 1024)


def pack_kernel(k_ref, v_ref, out_ref):
    for b in range(LOCAL):
        rows = slice(b * BLK, (b + 1) * BLK)
        k = k_ref[rows, :]
        out_ref[b, 0:BLK] = v_ref[rows, :]
        out_ref[b, BLK : 2 * BLK] = k[:, :128]
        low = k[:, 128:]
        out_ref[b, 2 * BLK :] = jnp.concatenate([low[:32], low[32:]], axis=1)


def pack(keys, values):
    return pl.pallas_call(
        pack_kernel,
        out_shape=jax.ShapeDtypeStruct((LOCAL, ROWS, 128), BF),
        compiler_params=params(),
        name="pack",
    )(keys, values)


def build_kernel(first, z_ref, req_ref, *refs):
    tables, out_ref = refs[:-1], refs[-1]
    c = pl.program_id(0)
    for d in range(out_ref.shape[1]):
        r = req_ref[c, first + d]

        @pl.when(r > 0)
        def _():
            if len(tables) > 1:
                out_ref[0, d] = tables[d][r - 1]
            else:
                out_ref[0, d] = tables[0][(z_ref[0] + d + 2) % tables[0].shape[0], r - 1]


def build(first, count, z, req, *tables):
    plane = req.shape[0]
    return pl.pallas_call(
        functools.partial(build_kernel, first),
        grid_spec=pltpu.PrefetchScalarGridSpec(
            num_scalar_prefetch=2,
            grid=(plane,),
            in_specs=[
                pl.BlockSpec(t.shape, functools.partial(lambda n, c, z, req: (0,) * n, t.ndim))
                for t in tables
            ],
            out_specs=pl.BlockSpec((1, count, ROWS, 128), lambda c, z, req: (c, 0, 0, 0)),
        ),
        out_shape=jax.ShapeDtypeStruct((plane, count, ROWS, 128), BF),
        compiler_params=params(),
        name="build",
    )(z, req, *tables)


def sum_block(first, d, req_ref, ret_ref, acc_ref):
    acc_ref[...] = jnp.zeros_like(acc_ref)
    for c in range(ret_ref.shape[0]):
        r = req_ref[c, first + d]

        @pl.when(r > 0)
        def _():
            acc_ref[r - 1] += ret_ref[c, 0].astype(F32)


def sum_near_kernel(z_ref, req_ref, ret_ref, out_ref, acc_ref):
    sum_block(0, pl.program_id(0), req_ref, ret_ref, acc_ref)
    out_ref[0] = acc_ref[...].astype(BF)


def sum_far_kernel(z_ref, req_ref, ret_ref, hold_ref, out_ref, held_ref, acc_ref):
    d = pl.program_id(0)
    far = d >= 3

    @pl.when(far)
    def _():
        sum_block(3, d - 3, req_ref, ret_ref, acc_ref)
        out_ref[0] = acc_ref[...].astype(BF)

    @pl.when(jnp.logical_not(far))
    def _():
        out_ref[0] = jnp.zeros_like(out_ref[0])


def far_step(depth, d):
    return jnp.where(d < 2, d, jnp.where(d == 2, depth - 1, d - 1))


def sum_near(z, req, returned):
    plane, count = returned.shape[:2]
    return pl.pallas_call(
        sum_near_kernel,
        grid_spec=pltpu.PrefetchScalarGridSpec(
            num_scalar_prefetch=2,
            grid=(count,),
            in_specs=[pl.BlockSpec((plane, 1, ROWS, 128), lambda d, z, req: (0, d, 0, 0))],
            out_specs=pl.BlockSpec((1, LOCAL, ROWS, 128), lambda d, z, req: (d, 0, 0, 0)),
            scratch_shapes=[pltpu.VMEM((LOCAL, ROWS, 128), F32)],
        ),
        out_shape=jax.ShapeDtypeStruct((count, LOCAL, ROWS, 128), BF),
        compiler_params=params(),
        name="sum_near",
    )(z, req, returned)


def sum_far(depth, z, req, returned, held):
    plane = returned.shape[0]
    return pl.pallas_call(
        sum_far_kernel,
        grid_spec=pltpu.PrefetchScalarGridSpec(
            num_scalar_prefetch=2,
            grid=(depth,),
            in_specs=[
                pl.BlockSpec(
                    (plane, 1, ROWS, 128), lambda d, z, req: (0, jnp.maximum(d - 3, 0), 0, 0)
                ),
                pl.BlockSpec(memory_space=pl.ANY),
            ],
            out_specs=[
                pl.BlockSpec(
                    (1, LOCAL, ROWS, 128),
                    lambda d, z, req: ((z[0] + far_step(depth, d)) % depth, 0, 0, 0),
                ),
                pl.BlockSpec(memory_space=pl.ANY),
            ],
            scratch_shapes=[pltpu.VMEM((LOCAL, ROWS, 128), F32)],
        ),
        out_shape=(
            jax.ShapeDtypeStruct((depth, LOCAL, ROWS, 128), BF),
            jax.ShapeDtypeStruct(held.shape, BF),
        ),
        input_output_aliases={3: 1},
        compiler_params=params(),
        name="sum_far",
    )(z, req, returned, held)


def finish_kernel(own_ref, *refs):
    got_refs, (dk_ref, dv_ref) = refs[:-2], refs[-2:]
    for b in range(LOCAL):
        rows = slice(b * BLK, (b + 1) * BLK)
        total = own_ref[b]
        for got_ref in got_refs:
            total = total + got_ref[b].astype(F32)
        dv_ref[rows, :] = total[0:BLK].astype(BF)
        low = total[2 * BLK :]
        low = jnp.concatenate([low[:, :64], low[:, 64:]], axis=0)
        dk_ref[rows, :] = jnp.concatenate([total[BLK : 2 * BLK], low], axis=1).astype(BF)


def finish(own, *got):
    return pl.pallas_call(
        finish_kernel,
        out_shape=(
            jax.ShapeDtypeStruct((LOCAL * BLK, DK), BF),
            jax.ShapeDtypeStruct((LOCAL * BLK, DV), BF),
        ),
        compiler_params=params(),
        name="finish",
    )(own, *got)


def dot(a, b, da, db):
    return lax.dot_general(a, b, (((da,), (db,)), ((), ())), preferred_element_type=F32)


def swap(x):
    return jnp.concatenate([x[:, 64:], x[:, :64]], axis=1)


def attend_kernel(
    src_ref,
    q_ref,
    do_ref,
    local_hbm,
    near_hbm,
    far_hbm,
    att_ref,
    dq_ref,
    part_near_hbm,
    part_far_hbm,
    own_ref,
    table,
    part,
    k_buf,
    v_buf,
    q_buf,
    do_buf,
    p_buf,
    pb_buf,
    dk_buf,
    dv_buf,
    sems,
):
    b = pl.program_id(0)
    n_near, n_far = near_hbm.shape[0], far_hbm.shape[0]
    n_remote = n_near + n_far
    scale = DK**-0.5
    half = BLK // 2
    group = SEL * half
    left = lax.broadcasted_iota(jnp.int32, (half, 128), 1) < 64

    @pl.when(b == 0)
    def _():
        places = ((near_hbm, 0, n_near), (far_hbm, n_near, n_far), (local_hbm, n_remote, LOCAL))
        copies = [
            pltpu.make_async_copy(ref, table.at[pl.ds(at, n)], sems.at[i])
            for i, (ref, at, n) in enumerate(places)
        ]
        for copy in copies:
            copy.start()
        own_ref[...] = jnp.zeros_like(own_ref)
        v_buf[:, 128:] = jnp.ones((2 * group, 128), BF)
        for copy in copies:
            copy.wait()

    key_id = lax.broadcasted_iota(jnp.int32, (half, 128), 0)
    query_id = lax.broadcasted_iota(jnp.int32, (half, 128), 1) % BLK
    none = jnp.zeros((half, 128), BF)
    masks = [
        jnp.where(key_id + g * half > query_id, NEG, 0.0).astype(BF) for g in range(2)
    ]
    for e in range(SEL):
        s = src_ref[b, e]
        mine = s == n_remote + b
        low = table[s, 2 * BLK :]
        for g in range(2):
            at = g * group + e * half
            rows = slice(at, at + half)
            v_buf[rows, 0:128] = table[s, g * half : (g + 1) * half]
            k_buf[rows, 0:128] = table[s, BLK + g * half : BLK + (g + 1) * half]
            mask = jnp.where(mine, masks[g], none)
            k_buf[rows, 128:] = jnp.where(left, low, mask) if g == 0 else jnp.where(left, mask, low)

    lane = lax.broadcasted_iota(jnp.int32, (BLK, 128), 1)
    first = lane < 64
    one_hot = (lax.broadcasted_iota(jnp.int32, (BLK, 128), 0) == lane % BLK).astype(BF)
    for h in range(0, HEADS, 2):
        t0, t1, t2 = (q_ref[:, h * DK + i * 128 : h * DK + (i + 1) * 128] for i in range(3))
        r1, r2 = swap(t1), swap(t2)
        for k, (high, low, swapped) in enumerate(((t0, t1, r1), (jnp.where(first, r1, r2), r2, t2))):
            rows = slice((h + k) * BLK, (h + k + 1) * BLK)
            for g in range(2):
                q_buf[g, rows, 0:128] = high
            q_buf[0, rows, 128:] = jnp.where(first, low, one_hot)
            q_buf[1, rows, 128:] = jnp.where(first, one_hot, swapped)

    groups = [slice(0, group), slice(group, 2 * group)]
    top = None
    for g in range(2):
        s = dot(k_buf[groups[g], :], q_buf[g], 1, 1)
        p_buf[groups[g], :] = s
        m = jnp.max(s, axis=0, keepdims=True)
        top = m if top is None else jnp.maximum(top, m)
    out_t = None
    for g in range(2):
        p = jnp.exp2((p_buf[groups[g], :] - top) * (scale * LOG2E))
        p_buf[groups[g], :] = p
        pb = p.astype(BF)
        pb_buf[groups[g], :] = pb
        o = dot(v_buf[groups[g], :], pb, 0, 0)
        out_t = o if out_t is None else out_t + o
    out = jnp.transpose(out_t)
    inverse = 1.0 / out[:, 128:129]
    att = (out[:, :128] * inverse).astype(BF)
    for h in range(HEADS):
        rows = slice(h * BLK, (h + 1) * BLK)
        att_ref[:, h * DV : (h + 1) * DV] = att[rows]
        do = (do_ref[:, h * DV : (h + 1) * DV].astype(F32) * inverse[rows]).astype(BF)
        delta = jnp.sum(do.astype(F32) * att[rows].astype(F32), axis=1, keepdims=True)
        high = delta.astype(BF)
        rest = delta - high.astype(F32)
        mid = rest.astype(BF)
        last = (rest - mid.astype(F32)).astype(BF)
        extra = jnp.where(
            lane == 0,
            high.astype(F32),
            jnp.where(lane == 1, mid.astype(F32), jnp.where(lane == 2, last.astype(F32), 0.0)),
        )
        do_buf[rows, 0:128] = do
        do_buf[rows, 128:] = (-extra).astype(BF)
    do_all = do_buf[...]
    dq_t = []
    for g in range(2):
        dp = dot(v_buf[groups[g], :], do_all, 1, 1)
        ds = (p_buf[groups[g], :] * dp).astype(BF)
        dv_buf[groups[g], :] = dot(pb_buf[groups[g], :], do_buf[:, 0:128], 1, 0)
        dk_buf[groups[g], :] = dot(ds, q_buf[g], 1, 0) * scale
        dq_t.append(dot(k_buf[groups[g], :], ds, 0, 0))
    for e in range(SEL):
        s = src_ref[b, e]
        at = jnp.minimum(s, n_remote)
        r1 = slice(e * half, (e + 1) * half)
        r2 = slice(group + e * half, group + (e + 1) * half)
        part[at, 0:half] = dv_buf[r1, :].astype(BF)
        part[at, half:BLK] = dv_buf[r2, :].astype(BF)
        part[at, BLK : BLK + half] = dk_buf[r1, 0:128].astype(BF)
        part[at, BLK + half : 2 * BLK] = dk_buf[r2, 0:128].astype(BF)
        part[at, 2 * BLK :] = jnp.where(left, dk_buf[r1, 128:], dk_buf[r2, 128:]).astype(BF)
    for e in range(SEL):
        s = src_ref[b, e]
        r1 = slice(e * half, (e + 1) * half)
        r2 = slice(group + e * half, group + (e + 1) * half)

        @pl.when(s >= n_remote)
        def _():
            i = s - n_remote
            own_ref[i, 0:half] += dv_buf[r1, :]
            own_ref[i, half:BLK] += dv_buf[r2, :]
            own_ref[i, BLK : BLK + half] += dk_buf[r1, 0:128]
            own_ref[i, BLK + half : 2 * BLK] += dk_buf[r2, 0:128]
            own_ref[i, 2 * BLK :] += jnp.where(left, dk_buf[r1, 128:], dk_buf[r2, 128:])

    high = jnp.transpose(dq_t[0][:128] + dq_t[1][:128]) * scale
    low = dq_t[0][128:192] + dq_t[1][192:]
    low = jnp.transpose(jnp.concatenate([low, low], axis=0)) * scale
    for h in range(0, HEADS, 2):
        even, odd = slice(h * BLK, (h + 1) * BLK), slice((h + 1) * BLK, (h + 2) * BLK)
        turned = swap(high[odd])
        parts = (high[even], jnp.where(first, low[even], turned), jnp.where(first, turned, low[odd]))
        for i, x in enumerate(parts):
            dq_ref[:, h * DK + i * 128 : h * DK + (i + 1) * 128] = x.astype(BF)

    @pl.when(b == LOCAL - 1)
    def _():
        places = ((part_near_hbm, 0, n_near), (part_far_hbm, n_near, n_far))
        copies = [
            pltpu.make_async_copy(part.at[pl.ds(at, n)], ref, sems.at[i])
            for i, (ref, at, n) in enumerate(places)
        ]
        for copy in copies:
            copy.start()
        for copy in copies:
            copy.wait()


def attend(src, queries, d_out, local, near, far):
    tokens = LOCAL * BLK
    keys = SEL * BLK
    rows = HEADS * BLK
    n_near, n_far = (x.shape[0] * x.shape[1] for x in (near, far))
    anywhere = pl.BlockSpec(memory_space=pl.ANY)
    attended, d_queries, part_near, part_far, own = pl.pallas_call(
        attend_kernel,
        grid_spec=pltpu.PrefetchScalarGridSpec(
            num_scalar_prefetch=1,
            grid=(LOCAL,),
            in_specs=[
                pl.BlockSpec((BLK, HEADS * DK), lambda b, src: (b, 0)),
                pl.BlockSpec((BLK, HEADS * DV), lambda b, src: (b, 0)),
                anywhere,
                anywhere,
                anywhere,
            ],
            out_specs=[
                pl.BlockSpec((BLK, HEADS * DV), lambda b, src: (b, 0)),
                pl.BlockSpec((BLK, HEADS * DK), lambda b, src: (b, 0)),
                anywhere,
                anywhere,
                pl.BlockSpec((LOCAL, ROWS, 128), lambda b, src: (0, 0, 0)),
            ],
            scratch_shapes=[
                pltpu.VMEM((n_near + n_far + LOCAL, ROWS, 128), BF),
                pltpu.VMEM((n_near + n_far + 1, ROWS, 128), BF),
                pltpu.VMEM((keys, 256), BF),
                pltpu.VMEM((keys, 256), BF),
                pltpu.VMEM((2, rows, 256), BF),
                pltpu.VMEM((rows, 256), BF),
                pltpu.VMEM((keys, rows), F32),
                pltpu.VMEM((keys, rows), BF),
                pltpu.VMEM((keys, 256), F32),
                pltpu.VMEM((keys, 128), F32),
                pltpu.SemaphoreType.DMA((3,)),
            ],
        ),
        out_shape=(
            jax.ShapeDtypeStruct((tokens, HEADS * DV), BF),
            jax.ShapeDtypeStruct((tokens, HEADS * DK), BF),
            jax.ShapeDtypeStruct((n_near, ROWS, 128), BF),
            jax.ShapeDtypeStruct((n_far, ROWS, 128), BF),
            jax.ShapeDtypeStruct((LOCAL, ROWS, 128), F32),
        ),
        compiler_params=params(),
        name="attend",
    )(
        src,
        queries,
        d_out,
        local,
        near.reshape(n_near, ROWS, 128),
        far.reshape(n_far, ROWS, 128),
    )
    return attended, d_queries, part_near.reshape(near.shape), part_far.reshape(far.shape), own


def shards(depth, plane, queries, keys, values, selected, d_out):
    me = lax.axis_index(("z", "y", "x"))
    z = lax.axis_index("z")
    seq_count = depth * plane
    per_half = LOCAL // 2
    half_index = selected // per_half
    is_late = half_index >= seq_count
    owners = jnp.where(is_late, 2 * seq_count - 1 - half_index, half_index)
    inner = selected % per_half + jnp.where(is_late, per_half, 0)
    remote = owners != me
    offset = (owners // plane - z + depth) % depth
    order = jnp.where(offset < 2, offset, jnp.where(offset == depth - 1, 2, offset + 1))
    in_plane = owners % plane
    slots = jnp.where(
        order < 3, in_plane * 3 + order, 3 * plane + in_plane * (depth - 3) + order - 3
    )
    src = jnp.where(remote, slots, seq_count + inner).astype(jnp.int32)
    flat = jnp.where(remote, in_plane * depth + order, -1).reshape(-1)
    hits = flat[:, None] == jnp.arange(seq_count, dtype=jnp.int32)[None, :]
    wanted = jnp.max(jnp.where(hits, inner.reshape(-1)[:, None] + 1, 0), axis=0)
    exchange = functools.partial(
        lax.all_to_all, axis_name=("y", "x"), split_axis=0, concat_axis=0, tiled=True
    )
    up = [(i, (i + 1) % depth) for i in range(depth)]
    down = [(i, (i - 1) % depth) for i in range(depth)]
    where_z = z.reshape(1).astype(jnp.int32)

    local = pack(keys, values)
    above = lax.ppermute(local, "z", down)
    below = lax.ppermute(local, "z", up)
    asked = exchange(wanted.reshape(plane, 1, depth)).reshape(plane, depth)
    column = lax.all_gather(local, "z")
    near = exchange(build(0, 3, where_z, asked, local, above, below))
    far = exchange(build(3, depth - 3, where_z, asked, column))
    attended, d_queries, part_near, part_far, own = attend(src, queries, d_out, local, near, far)
    back_far = exchange(part_far)
    far_sums, part_near = sum_far(depth, where_z, asked, back_far, part_near)
    mine = lax.psum_scatter(far_sums, "z", scatter_dimension=0)
    near_sums = sum_near(where_z, asked, exchange(part_near))
    from_below = lax.ppermute(near_sums[1], "z", up)
    from_above = lax.ppermute(near_sums[2], "z", down)
    d_keys, d_values = finish(own, near_sums[0], from_below, from_above, mine)
    return attended, d_queries, d_keys, d_values


def solution(mesh):
    grid = Mesh(mesh.devices.reshape(SIDES + (-1,)), ("z", "y", "x", "grp"))
    spec = P(("z", "y", "x"), "grp")
    return jax.shard_map(
        functools.partial(shards, SIDES[0], SIDES[1] * SIDES[2]),
        mesh=grid,
        in_specs=(spec,) * 5,
        out_specs=(spec,) * 4,
        check_vma=False,
    )
```

```python
import functools

import jax
import jax.numpy as jnp
from jax import lax
from jax.experimental import pallas as pl
from jax.experimental.pallas import tpu as pltpu
from jax.sharding import Mesh, PartitionSpec as P

BLK = 64
SEL = 16
HEADS = 8
DK = 192
DV = 128
ROWS = 160
SIDES = (8, 4, 4)
LOCAL = 8
LOG2E = 1.4426950408889634
NEG = -1e30
BF = jnp.bfloat16
F32 = jnp.float32


def params(mib=56):
    return pltpu.CompilerParams(vmem_limit_bytes=mib * 1024 * 1024)


def pack_kernel(k_ref, v_ref, out_ref):
    for b in range(0, LOCAL, 2):
        pair = jnp.transpose(k_ref[:, b * BLK : (b + 2) * BLK])
        for i in range(2):
            k = pair[i * BLK : (i + 1) * BLK]
            out_ref[b + i, 0:BLK] = v_ref[(b + i) * BLK : (b + i + 1) * BLK, :]
            out_ref[b + i, BLK : 2 * BLK] = k[:, :128]
            low = k[:, 128:]
            out_ref[b + i, 2 * BLK :] = jnp.concatenate([low[:32], low[32:]], axis=1)


def pack(keys_t, values):
    return pl.pallas_call(
        pack_kernel,
        out_shape=jax.ShapeDtypeStruct((LOCAL, ROWS, 128), BF),
        compiler_params=params(),
        name="pack",
    )(keys_t, values)


def build_kernel(first, z_ref, req_ref, *refs):
    tables, out_hbm = refs[: (len(refs) - 3) // 2], refs[(len(refs) - 3) // 2]
    held, (load_sems, sems) = refs[-2 - len(tables) : -2], refs[-2:]
    plane, count = out_hbm.shape[:2]
    loads = [
        pltpu.make_async_copy(t, h, load_sems.at[i]) for i, (t, h) in enumerate(zip(tables, held))
    ]
    for load in loads:
        load.start()
    sends = []
    for d in range(count):
        if d < len(loads):
            loads[d].wait()
        for c in range(plane):
            r = jnp.maximum(req_ref[c, first + d], 1) - 1
            if len(held) > 1:
                block = held[d].at[r]
            else:
                block = held[0].at[(z_ref[0] + d + 2) % held[0].shape[0], r]
            sends.append(pltpu.make_async_copy(block, out_hbm.at[c, d], sems.at[c, d]))
            sends[-1].start()
    for send in sends:
        send.wait()


def build(first, count, z, req, *tables):
    plane = req.shape[0]
    anywhere = pl.BlockSpec(memory_space=pl.ANY)
    return pl.pallas_call(
        functools.partial(build_kernel, first),
        grid_spec=pltpu.PrefetchScalarGridSpec(
            num_scalar_prefetch=2,
            grid=(1,),
            in_specs=[anywhere] * len(tables),
            out_specs=anywhere,
            scratch_shapes=[pltpu.VMEM(t.shape, BF) for t in tables]
            + [pltpu.SemaphoreType.DMA((len(tables),)), pltpu.SemaphoreType.DMA((plane, count))],
        ),
        out_shape=jax.ShapeDtypeStruct((plane, count, ROWS, 128), BF),
        compiler_params=params(),
        name="build",
    )(z, req, *tables)


def sum_blocks(first, req_ref, ret_hbm, buf, acc, staged, in_sems, out_sems, target):
    plane, count = ret_hbm.shape[:2]
    loads = [
        pltpu.make_async_copy(ret_hbm.at[:, d], buf.at[d], in_sems.at[d]) for d in range(count)
    ]
    for load in loads:
        load.start()
    stores = []
    for d in range(count):
        loads[d].wait()
        acc[...] = jnp.zeros_like(acc)
        for c in range(plane):
            acc[req_ref[c, first + d]] += buf[d, c].astype(F32)
        staged[d] = acc[1:].astype(BF)
        stores.append(pltpu.make_async_copy(staged.at[d], target(d), out_sems.at[d]))
        stores[-1].start()
    return stores


def sum_near_kernel(req_ref, ret_hbm, *refs):
    outs, (buf, acc, staged, in_sems, out_sems) = refs[:-5], refs[-5:]
    for store in sum_blocks(
        0, req_ref, ret_hbm, buf, acc, staged, in_sems, out_sems, lambda d: outs[d]
    ):
        store.wait()


def sum_far_kernel(
    z_ref, req_ref, ret_hbm, hold_ref, out_hbm, held_ref, buf, acc, staged, in_sems, out_sems
):
    depth, count = out_hbm.shape[0], ret_hbm.shape[1]
    near = depth - count
    z = z_ref[0]
    staged[count] = jnp.zeros_like(staged[count])
    zeros = [
        pltpu.make_async_copy(
            staged.at[count], out_hbm.at[(z + depth + i - 1) % depth], out_sems.at[count + i]
        )
        for i in range(near)
    ]
    for zero in zeros:
        zero.start()
    for store in zeros + sum_blocks(
        near,
        req_ref,
        ret_hbm,
        buf,
        acc,
        staged,
        in_sems,
        out_sems,
        lambda d: out_hbm.at[(z + d + 2) % depth],
    ):
        store.wait()


def sum_scratch(plane, count, depth):
    return [
        pltpu.VMEM((count, plane, ROWS, 128), BF),
        pltpu.VMEM((LOCAL + 1, ROWS, 128), F32),
        pltpu.VMEM((count + 1, LOCAL, ROWS, 128), BF),
        pltpu.SemaphoreType.DMA((count,)),
        pltpu.SemaphoreType.DMA((depth,)),
    ]


def sum_near(req, returned):
    plane, count = returned.shape[:2]
    anywhere = pl.BlockSpec(memory_space=pl.ANY)
    return pl.pallas_call(
        sum_near_kernel,
        grid_spec=pltpu.PrefetchScalarGridSpec(
            num_scalar_prefetch=1,
            grid=(1,),
            in_specs=[anywhere],
            out_specs=[anywhere] * count,
            scratch_shapes=sum_scratch(plane, count, count),
        ),
        out_shape=[jax.ShapeDtypeStruct((LOCAL, ROWS, 128), BF)] * count,
        compiler_params=params(),
        name="sum_near",
    )(req, returned)


def sum_far(depth, z, req, returned, held):
    plane, count = returned.shape[:2]
    anywhere = pl.BlockSpec(memory_space=pl.ANY)
    return pl.pallas_call(
        sum_far_kernel,
        grid_spec=pltpu.PrefetchScalarGridSpec(
            num_scalar_prefetch=2,
            grid=(1,),
            in_specs=[anywhere, anywhere],
            out_specs=[anywhere, anywhere],
            scratch_shapes=sum_scratch(plane, count, depth),
        ),
        out_shape=(
            jax.ShapeDtypeStruct((depth, LOCAL, ROWS, 128), BF),
            jax.ShapeDtypeStruct(held.shape, BF),
        ),
        input_output_aliases={3: 1},
        compiler_params=params(),
        name="sum_far",
    )(z, req, returned, held)


def finish_kernel(own_ref, *refs):
    got_refs, (dk_ref, dv_ref) = refs[:-2], refs[-2:]
    for b in range(0, LOCAL, 2):
        pair = []
        for i in range(b, b + 2):
            total = own_ref[i]
            for got_ref in got_refs:
                total = total + got_ref[i].astype(F32)
            dv_ref[i * BLK : (i + 1) * BLK, :] = total[0:BLK].astype(BF)
            low = total[2 * BLK :]
            low = jnp.concatenate([low[:, :64], low[:, 64:]], axis=0)
            pair.append(jnp.concatenate([total[BLK : 2 * BLK], low], axis=1))
        pair = jnp.concatenate(pair, axis=0)
        dk_ref[:, b * BLK : (b + 2) * BLK] = jnp.transpose(pair).astype(BF)


def finish(own, *got):
    return pl.pallas_call(
        finish_kernel,
        out_shape=(
            jax.ShapeDtypeStruct((DK, LOCAL * BLK), BF),
            jax.ShapeDtypeStruct((LOCAL * BLK, DV), BF),
        ),
        compiler_params=params(),
        name="finish",
    )(own, *got)


def dot(a, b, da, db):
    return lax.dot_general(a, b, (((da,), (db,)), ((), ())), preferred_element_type=F32)


def swap(x):
    return jnp.concatenate([x[:, 64:], x[:, :64]], axis=1)


HALF_BLK = BLK // 2
GROUP = SEL * HALF_BLK
PAIR = 4


def lane_ids(rows):
    return lax.broadcasted_iota(jnp.int32, (rows, 128), 1)


def attend_kernel(
    src_ref,
    q_ref,
    do_ref,
    local_hbm,
    near_hbm,
    far_hbm,
    att_ref,
    dq_ref,
    part_near_hbm,
    part_far_hbm,
    own_ref,
    table,
    part,
    k_bufs,
    v_bufs,
    q_bufs,
    do_bufs,
    p_bufs,
    pb_bufs,
    dk_bufs,
    dv_bufs,
    sems,
):
    step = pl.program_id(0)
    n_near, n_far = near_hbm.shape[0], far_hbm.shape[0]
    n_remote = n_near + n_far
    scale = DK**-0.5
    left = lane_ids(HALF_BLK) < 64
    lane = lane_ids(BLK)
    first = lane < 64
    groups = [slice(0, GROUP), slice(GROUP, 2 * GROUP)]

    @pl.when(step == 0)
    def _():
        places = ((near_hbm, 0, n_near), (far_hbm, n_near, n_far), (local_hbm, n_remote, LOCAL))
        copies = [
            pltpu.make_async_copy(ref, table.at[pl.ds(at, n)], sems.at[i])
            for i, (ref, at, n) in enumerate(places)
        ]
        for copy in copies:
            copy.start()
        own_ref[...] = jnp.zeros_like(own_ref)
        for i in range(PAIR):
            v_bufs[i, :, 128:] = jnp.ones((2 * GROUP, 128), BF)
        for copy in copies:
            copy.wait()

    class Block:
        def __init__(self, i):
            self.i, self.b = i, step * PAIR + i
            self.rows = slice(i * BLK, (i + 1) * BLK)
            self.k, self.v, self.q, self.do = (x.at[i] for x in (k_bufs, v_bufs, q_bufs, do_bufs))
            self.p, self.pb, self.dk, self.dv = (x.at[i] for x in (p_bufs, pb_bufs, dk_bufs, dv_bufs))

        def place_keys(self):
            key_id = lax.broadcasted_iota(jnp.int32, (HALF_BLK, 128), 0)
            query_id = lane_ids(HALF_BLK) % BLK
            none = jnp.zeros((HALF_BLK, 128), BF)
            masks = [
                jnp.where(key_id + g * HALF_BLK > query_id, NEG, 0.0).astype(BF) for g in range(2)
            ]
            for e in range(SEL):
                s = src_ref[self.b, e]
                mine = s == n_remote + self.b
                low = table[s, 2 * BLK :]
                for g in range(2):
                    at = g * GROUP + e * HALF_BLK
                    rows = slice(at, at + HALF_BLK)
                    self.v[rows, 0:128] = table[s, g * HALF_BLK : (g + 1) * HALF_BLK]
                    self.k[rows, 0:128] = table[s, BLK + g * HALF_BLK : BLK + (g + 1) * HALF_BLK]
                    mask = jnp.where(mine, masks[g], none)
                    both = (low, mask) if g == 0 else (mask, low)
                    self.k[rows, 128:] = jnp.where(left, *both)

        def place_queries(self):
            one_hot = (lax.broadcasted_iota(jnp.int32, (BLK, 128), 0) == lane % BLK).astype(BF)
            for h in range(0, HEADS, 2):
                t0, t1, t2 = (
                    q_ref[self.rows, h * DK + i * 128 : h * DK + (i + 1) * 128] for i in range(3)
                )
                r1, r2 = swap(t1), swap(t2)
                for k, (high, low, swapped) in enumerate(
                    ((t0, t1, r1), (jnp.where(first, r1, r2), r2, t2))
                ):
                    rows = slice((h + k) * BLK, (h + k + 1) * BLK)
                    for g in range(2):
                        self.q[g, rows, 0:128] = high
                    self.q[0, rows, 128:] = jnp.where(first, low, one_hot)
                    self.q[1, rows, 128:] = jnp.where(first, one_hot, swapped)

        def score(self):
            self.top = None
            for g, rows in enumerate(groups):
                s = dot(self.k[rows, :], self.q[g], 1, 1)
                self.p[rows, :] = s
                m = jnp.max(s, axis=0, keepdims=True)
                self.top = m if self.top is None else jnp.maximum(self.top, m)

        def weigh(self):
            self.out_t = None
            for rows in groups:
                p = jnp.exp2((self.p[rows, :] - self.top) * (scale * LOG2E))
                self.p[rows, :] = p
                pb = p.astype(BF)
                self.pb[rows, :] = pb
                o = dot(self.v[rows, :], pb, 0, 0)
                self.out_t = o if self.out_t is None else self.out_t + o

        def output(self):
            out = jnp.transpose(self.out_t[: DV + 8])
            inverse = 1.0 / out[:, 128:129]
            att = (out[:, :128] * inverse).astype(BF)
            for h in range(HEADS):
                rows = slice(h * BLK, (h + 1) * BLK)
                cols = slice(h * DV, (h + 1) * DV)
                att_ref[self.rows, cols] = att[rows]
                do = (do_ref[self.rows, cols].astype(F32) * inverse[rows]).astype(BF)
                delta = jnp.sum(do.astype(F32) * att[rows].astype(F32), axis=1, keepdims=True)
                delta = jnp.broadcast_to(-delta, (BLK, 128))
                high = delta.astype(BF).astype(F32)
                rest = delta - high
                mid = rest.astype(BF).astype(F32)
                extra = jnp.where(
                    lane == 0, high, jnp.where(lane == 1, mid, jnp.where(lane == 2, rest - mid, 0.0))
                )
                self.do[rows, 0:128] = do
                self.do[rows, 128:] = extra.astype(BF)

        def backward(self):
            do_all = self.do[...]
            self.dq_t = []
            for g, rows in enumerate(groups):
                dp = dot(self.v[rows, :], do_all, 1, 1)
                ds = (self.p[rows, :] * dp).astype(BF)
                self.dv[rows, :] = dot(self.pb[rows, :], self.do[:, 0:128], 1, 0)
                self.dk[rows, :] = dot(ds, self.q[g], 1, 0) * scale
                self.dq_t.append(dot(self.k[rows, :], ds, 0, 0))

        def packed(self, e):
            r1 = slice(e * HALF_BLK, (e + 1) * HALF_BLK)
            r2 = slice(GROUP + e * HALF_BLK, GROUP + (e + 1) * HALF_BLK)
            return (
                (slice(0, HALF_BLK), self.dv[r1, :]),
                (slice(HALF_BLK, BLK), self.dv[r2, :]),
                (slice(BLK, BLK + HALF_BLK), self.dk[r1, 0:128]),
                (slice(BLK + HALF_BLK, 2 * BLK), self.dk[r2, 0:128]),
                (slice(2 * BLK, ROWS), jnp.where(left, self.dk[r1, 128:], self.dk[r2, 128:])),
            )

        def store_parts(self):
            for e in range(SEL):
                at = jnp.minimum(src_ref[self.b, e], n_remote)
                for rows, x in self.packed(e):
                    part[at, rows] = x.astype(BF)

        def add_own(self):
            for rows, x in self.packed(0):
                own_ref[self.b, rows] += x
            for e in range(1, SEL):
                s = src_ref[self.b, e]

                @pl.when(s >= n_remote)
                def _():
                    for rows, x in self.packed(e):
                        own_ref[s - n_remote, rows] += x

        def query_grads(self):
            high = jnp.transpose(self.dq_t[0][:128] + self.dq_t[1][:128]) * scale
            low = self.dq_t[0][128:192] + self.dq_t[1][192:]
            low = jnp.transpose(jnp.concatenate([low, low], axis=0)) * scale
            for h in range(0, HEADS, 2):
                even, odd = slice(h * BLK, (h + 1) * BLK), slice((h + 1) * BLK, (h + 2) * BLK)
                turned = swap(high[odd])
                parts = (
                    high[even],
                    jnp.where(first, low[even], turned),
                    jnp.where(first, turned, low[odd]),
                )
                for i, x in enumerate(parts):
                    dq_ref[self.rows, h * DK + i * 128 : h * DK + (i + 1) * 128] = x.astype(BF)

    blocks = [Block(i) for i in range(PAIR)]
    for block in blocks:
        block.place_keys()
    for block in blocks:
        block.place_queries()
    for block in blocks:
        block.score()
    for block in blocks:
        block.weigh()
    for block in blocks:
        block.output()
    for block in blocks:
        block.backward()
    for block in blocks:
        block.store_parts()
    for block in blocks:
        block.query_grads()
    for block in blocks:
        block.add_own()

    @pl.when(step == LOCAL // PAIR - 1)
    def _():
        places = ((part_near_hbm, 0, n_near), (part_far_hbm, n_near, n_far))
        copies = [
            pltpu.make_async_copy(part.at[pl.ds(at, n)], ref, sems.at[i])
            for i, (ref, at, n) in enumerate(places)
        ]
        for copy in copies:
            copy.start()
        for copy in copies:
            copy.wait()


def attend(src, queries, d_out, local, near, far):
    tokens = LOCAL * BLK
    keys = SEL * BLK
    rows = HEADS * BLK
    n_near, n_far = (x.shape[0] * x.shape[1] for x in (near, far))
    anywhere = pl.BlockSpec(memory_space=pl.ANY)
    attended, d_queries, part_near, part_far, own = pl.pallas_call(
        attend_kernel,
        grid_spec=pltpu.PrefetchScalarGridSpec(
            num_scalar_prefetch=1,
            grid=(LOCAL // PAIR,),
            in_specs=[
                pl.BlockSpec((PAIR * BLK, HEADS * DK), lambda b, src: (b, 0)),
                pl.BlockSpec((PAIR * BLK, HEADS * DV), lambda b, src: (b, 0)),
                anywhere,
                anywhere,
                anywhere,
            ],
            out_specs=[
                pl.BlockSpec((PAIR * BLK, HEADS * DV), lambda b, src: (b, 0)),
                pl.BlockSpec((PAIR * BLK, HEADS * DK), lambda b, src: (b, 0)),
                anywhere,
                anywhere,
                pl.BlockSpec((LOCAL, ROWS, 128), lambda b, src: (0, 0, 0)),
            ],
            scratch_shapes=[
                pltpu.VMEM((n_near + n_far + LOCAL, ROWS, 128), BF),
                pltpu.VMEM((n_near + n_far + 1, ROWS, 128), BF),
                pltpu.VMEM((PAIR, keys, 256), BF),
                pltpu.VMEM((PAIR, keys, 256), BF),
                pltpu.VMEM((PAIR, 2, rows, 256), BF),
                pltpu.VMEM((PAIR, rows, 256), BF),
                pltpu.VMEM((PAIR, keys, rows), F32),
                pltpu.VMEM((PAIR, keys, rows), BF),
                pltpu.VMEM((PAIR, keys, 256), F32),
                pltpu.VMEM((PAIR, keys, 128), F32),
                pltpu.SemaphoreType.DMA((3,)),
            ],
        ),
        out_shape=(
            jax.ShapeDtypeStruct((tokens, HEADS * DV), BF),
            jax.ShapeDtypeStruct((tokens, HEADS * DK), BF),
            jax.ShapeDtypeStruct((n_near, ROWS, 128), BF),
            jax.ShapeDtypeStruct((n_far, ROWS, 128), BF),
            jax.ShapeDtypeStruct((LOCAL, ROWS, 128), F32),
        ),
        compiler_params=params(),
        name="attend",
    )(
        src,
        queries,
        d_out,
        local,
        near.reshape(n_near, ROWS, 128),
        far.reshape(n_far, ROWS, 128),
    )
    return attended, d_queries, part_near.reshape(near.shape), part_far.reshape(far.shape), own


def shards(depth, plane, queries, keys, values, selected, d_out):
    me = lax.axis_index(("z", "y", "x"))
    z = lax.axis_index("z")
    seq_count = depth * plane
    per_half = LOCAL // 2
    half_index = selected // per_half
    is_late = half_index >= seq_count
    owners = jnp.where(is_late, 2 * seq_count - 1 - half_index, half_index)
    inner = selected % per_half + jnp.where(is_late, per_half, 0)
    remote = owners != me
    offset = (owners // plane - z + depth) % depth
    order = jnp.where(offset < 2, offset, jnp.where(offset == depth - 1, 2, offset + 1))
    in_plane = owners % plane
    slots = jnp.where(
        order < 3, in_plane * 3 + order, 3 * plane + in_plane * (depth - 3) + order - 3
    )
    src = jnp.where(remote, slots, seq_count + inner).astype(jnp.int32)
    flat = jnp.where(remote, in_plane * depth + order, -1).reshape(-1)
    hits = flat[:, None] == jnp.arange(seq_count, dtype=jnp.int32)[None, :]
    wanted = jnp.max(jnp.where(hits, inner.reshape(-1)[:, None] + 1, 0), axis=0)
    exchange = functools.partial(
        lax.all_to_all, axis_name=("y", "x"), split_axis=0, concat_axis=0, tiled=True
    )
    up = [(i, (i + 1) % depth) for i in range(depth)]
    down = [(i, (i - 1) % depth) for i in range(depth)]
    where_z = z.reshape(1).astype(jnp.int32)

    local = pack(keys.T, values)
    above = lax.ppermute(local, "z", down)
    below = lax.ppermute(local, "z", up)
    asked = exchange(wanted.reshape(plane, 1, depth)).reshape(plane, depth)
    column = lax.all_gather(local, "z")
    near = exchange(build(0, 3, where_z, asked, local, above, below))
    far = exchange(build(3, depth - 3, where_z, asked, column))
    attended, d_queries, part_near, part_far, own = attend(src, queries, d_out, local, near, far)
    back_far = exchange(part_far)
    far_sums, part_near = sum_far(depth, where_z, asked, back_far, part_near)
    mine = lax.psum_scatter(far_sums, "z", scatter_dimension=0)
    here, to_above, to_below = sum_near(asked, exchange(part_near))
    from_below = lax.ppermute(to_above, "z", up)
    from_above = lax.ppermute(to_below, "z", down)
    d_keys_t, d_values = finish(own, here, from_below, from_above, mine)
    return attended, d_queries, d_keys_t.T, d_values


def solution(mesh):
    grid = Mesh(mesh.devices.reshape(SIDES + (-1,)), ("z", "y", "x", "grp"))
    spec = P(("z", "y", "x"), "grp")
    return jax.shard_map(
        functools.partial(shards, SIDES[0], SIDES[1] * SIDES[2]),
        mesh=grid,
        in_specs=(spec,) * 5,
        out_specs=(spec,) * 4,
        check_vma=False,
    )
```

```python
import functools

import jax
import jax.numpy as jnp
from jax import lax
from jax.experimental import pallas as pl
from jax.experimental.pallas import tpu as pltpu
from jax.sharding import Mesh, PartitionSpec as P

BLK = 64
SEL = 16
HEADS = 8
DK = 192
DV = 128
ROWS = 160
SIDES = (8, 4, 4)
LOCAL = 8
LOG2E = 1.4426950408889634
NEG = -1e30
BF = jnp.bfloat16
F32 = jnp.float32


def params(mib=56):
    return pltpu.CompilerParams(vmem_limit_bytes=mib * 1024 * 1024)


def pack_kernel(k_ref, v_ref, out_ref):
    for b in range(0, LOCAL, 2):
        pair = jnp.transpose(k_ref[:, b * BLK : (b + 2) * BLK])
        for i in range(2):
            k = pair[i * BLK : (i + 1) * BLK]
            out_ref[b + i, 0:BLK] = v_ref[(b + i) * BLK : (b + i + 1) * BLK, :]
            out_ref[b + i, BLK : 2 * BLK] = k[:, :128]
            low = k[:, 128:]
            out_ref[b + i, 2 * BLK :] = jnp.concatenate([low[:32], low[32:]], axis=1)


def pack(keys_t, values):
    return pl.pallas_call(
        pack_kernel,
        out_shape=jax.ShapeDtypeStruct((LOCAL, ROWS, 128), BF),
        compiler_params=params(),
        name="pack",
    )(keys_t, values)


def build_kernel(first, z_ref, req_ref, *refs):
    tables, out_hbm = refs[: (len(refs) - 3) // 2], refs[(len(refs) - 3) // 2]
    held, (load_sems, sems) = refs[-2 - len(tables) : -2], refs[-2:]
    plane, count = out_hbm.shape[:2]
    loads = [
        pltpu.make_async_copy(t, h, load_sems.at[i]) for i, (t, h) in enumerate(zip(tables, held))
    ]
    for load in loads:
        load.start()
    sends = []
    for d in range(count):
        if d < len(loads):
            loads[d].wait()
        for c in range(plane):
            r = jnp.maximum(req_ref[c, first + d], 1) - 1
            if len(held) > 1:
                block = held[d].at[r]
            else:
                block = held[0].at[(z_ref[0] + d + 2) % held[0].shape[0], r]
            sends.append(pltpu.make_async_copy(block, out_hbm.at[c, d], sems.at[c, d]))
            sends[-1].start()
    for send in sends:
        send.wait()


def build(first, count, z, req, *tables):
    plane = req.shape[0]
    anywhere = pl.BlockSpec(memory_space=pl.ANY)
    return pl.pallas_call(
        functools.partial(build_kernel, first),
        grid_spec=pltpu.PrefetchScalarGridSpec(
            num_scalar_prefetch=2,
            grid=(1,),
            in_specs=[anywhere] * len(tables),
            out_specs=anywhere,
            scratch_shapes=[pltpu.VMEM(t.shape, BF) for t in tables]
            + [pltpu.SemaphoreType.DMA((len(tables),)), pltpu.SemaphoreType.DMA((plane, count))],
        ),
        out_shape=jax.ShapeDtypeStruct((plane, count, ROWS, 128), BF),
        compiler_params=params(),
        name="build",
    )(z, req, *tables)


def sum_blocks(first, req_ref, ret_hbm, buf, acc, staged, in_sems, out_sems, target):
    plane, count = ret_hbm.shape[:2]
    loads = [
        pltpu.make_async_copy(ret_hbm.at[:, d], buf.at[d], in_sems.at[d]) for d in range(count)
    ]
    for load in loads:
        load.start()
    stores = []
    for d in range(count):
        loads[d].wait()
        acc[...] = jnp.zeros_like(acc)
        for c in range(plane):
            acc[req_ref[c, first + d]] += buf[d, c].astype(F32)
        staged[d] = acc[1:].astype(BF)
        stores.append(pltpu.make_async_copy(staged.at[d], target(d), out_sems.at[d]))
        stores[-1].start()
    return stores


def sum_near_kernel(first, req_ref, ret_hbm, *refs):
    outs, (buf, acc, staged, in_sems, out_sems) = refs[:-5], refs[-5:]
    for store in sum_blocks(
        first, req_ref, ret_hbm, buf, acc, staged, in_sems, out_sems, lambda d: outs[d]
    ):
        store.wait()


def sum_far_kernel(
    z_ref, req_ref, ret_hbm, out_hbm, buf, acc, staged, in_sems, out_sems
):
    depth, count = out_hbm.shape[0], ret_hbm.shape[1]
    near = depth - count
    z = z_ref[0]
    staged[count] = jnp.zeros_like(staged[count])
    zeros = [
        pltpu.make_async_copy(
            staged.at[count], out_hbm.at[(z + depth + i - 1) % depth], out_sems.at[count + i]
        )
        for i in range(near)
    ]
    for zero in zeros:
        zero.start()
    for store in zeros + sum_blocks(
        near,
        req_ref,
        ret_hbm,
        buf,
        acc,
        staged,
        in_sems,
        out_sems,
        lambda d: out_hbm.at[(z + d + 2) % depth],
    ):
        store.wait()


def sum_scratch(plane, count, depth):
    return [
        pltpu.VMEM((count, plane, ROWS, 128), BF),
        pltpu.VMEM((LOCAL + 1, ROWS, 128), F32),
        pltpu.VMEM((count + 1, LOCAL, ROWS, 128), BF),
        pltpu.SemaphoreType.DMA((count,)),
        pltpu.SemaphoreType.DMA((depth,)),
    ]


def sum_near(first, req, returned):
    plane, count = returned.shape[:2]
    anywhere = pl.BlockSpec(memory_space=pl.ANY)
    return pl.pallas_call(
        functools.partial(sum_near_kernel, first),
        grid_spec=pltpu.PrefetchScalarGridSpec(
            num_scalar_prefetch=1,
            grid=(1,),
            in_specs=[anywhere],
            out_specs=[anywhere] * count,
            scratch_shapes=sum_scratch(plane, count, count),
        ),
        out_shape=[jax.ShapeDtypeStruct((LOCAL, ROWS, 128), BF)] * count,
        compiler_params=params(),
        name="sum_near",
    )(req, returned)


def sum_far(depth, z, req, returned):
    plane, count = returned.shape[:2]
    anywhere = pl.BlockSpec(memory_space=pl.ANY)
    return pl.pallas_call(
        sum_far_kernel,
        grid_spec=pltpu.PrefetchScalarGridSpec(
            num_scalar_prefetch=2,
            grid=(1,),
            in_specs=[anywhere],
            out_specs=anywhere,
            scratch_shapes=sum_scratch(plane, count, depth),
        ),
        out_shape=jax.ShapeDtypeStruct((depth, LOCAL, ROWS, 128), BF),
        compiler_params=params(),
        name="sum_far",
    )(z, req, returned)


def finish_kernel(own_ref, *refs):
    got_refs, (dk_ref, dv_ref) = refs[:-2], refs[-2:]
    for b in range(0, LOCAL, 2):
        pair = []
        for i in range(b, b + 2):
            total = own_ref[i]
            for got_ref in got_refs:
                total = total + got_ref[i].astype(F32)
            dv_ref[i * BLK : (i + 1) * BLK, :] = total[0:BLK].astype(BF)
            low = total[2 * BLK :]
            low = jnp.concatenate([low[:, :64], low[:, 64:]], axis=0)
            pair.append(jnp.concatenate([total[BLK : 2 * BLK], low], axis=1))
        pair = jnp.concatenate(pair, axis=0)
        dk_ref[:, b * BLK : (b + 2) * BLK] = jnp.transpose(pair).astype(BF)


def finish(own, *got):
    return pl.pallas_call(
        finish_kernel,
        out_shape=(
            jax.ShapeDtypeStruct((DK, LOCAL * BLK), BF),
            jax.ShapeDtypeStruct((LOCAL * BLK, DV), BF),
        ),
        compiler_params=params(),
        name="finish",
    )(own, *got)


def dot(a, b, da, db):
    return lax.dot_general(a, b, (((da,), (db,)), ((), ())), preferred_element_type=F32)


def swap(x):
    return jnp.concatenate([x[:, 64:], x[:, :64]], axis=1)


HALF_BLK = BLK // 2
GROUP = SEL * HALF_BLK
PAIR = 4


def lane_ids(rows):
    return lax.broadcasted_iota(jnp.int32, (rows, 128), 1)


def attend_kernel(
    src_ref,
    q_ref,
    do_ref,
    local_hbm,
    near_hbm,
    far_hbm,
    att_ref,
    dq_ref,
    part_here_hbm,
    part_side_hbm,
    part_far_hbm,
    own_ref,
    table,
    part,
    k_bufs,
    v_bufs,
    q_bufs,
    do_bufs,
    p_bufs,
    pb_bufs,
    dk_bufs,
    dv_bufs,
    sems,
):
    step = pl.program_id(0)
    plane, n_far = near_hbm.shape[0], far_hbm.shape[0]
    n_near = plane * near_hbm.shape[1]
    n_remote = n_near + n_far
    scale = DK**-0.5
    left = lane_ids(HALF_BLK) < 64
    lane = lane_ids(BLK)
    first = lane < 64
    groups = [slice(0, GROUP), slice(GROUP, 2 * GROUP)]

    loads = [(near_hbm.at[:, d], d * plane, plane) for d in range(near_hbm.shape[1])]
    loads += [(local_hbm, n_remote, LOCAL), (far_hbm, n_near, n_far)]
    loads = [
        pltpu.make_async_copy(ref, table.at[pl.ds(at, n)], sems.at[i])
        for i, (ref, at, n) in enumerate(loads)
    ]
    stores = [(part_far_hbm, n_near, n_far), (part_here_hbm, 0, plane)]
    stores += [
        (part_side_hbm.at[:, d], (d + 1) * plane, plane) for d in range(part_side_hbm.shape[1])
    ]
    stores = [
        pltpu.make_async_copy(part.at[pl.ds(at, n)], ref, sems.at[i])
        for i, (ref, at, n) in enumerate(stores)
    ]

    @pl.when(step == 0)
    def _():
        for load in loads:
            load.start()
        own_ref[...] = jnp.zeros_like(own_ref)
        for i in range(PAIR):
            v_bufs[i, :, 128:] = jnp.ones((2 * GROUP, 128), BF)

    class Block:
        def __init__(self, i):
            self.i, self.b = i, step * PAIR + i
            self.rows = slice(i * BLK, (i + 1) * BLK)
            self.k, self.v, self.q, self.do = (x.at[i] for x in (k_bufs, v_bufs, q_bufs, do_bufs))
            self.p, self.pb, self.dk, self.dv = (x.at[i] for x in (p_bufs, pb_bufs, dk_bufs, dv_bufs))

        def place_keys(self):
            key_id = lax.broadcasted_iota(jnp.int32, (HALF_BLK, 128), 0)
            query_id = lane_ids(HALF_BLK) % BLK
            none = jnp.zeros((HALF_BLK, 128), BF)
            masks = [
                jnp.where(key_id + g * HALF_BLK > query_id, NEG, 0.0).astype(BF) for g in range(2)
            ]
            for e in range(SEL):
                s = src_ref[self.b, e]
                mine = s == n_remote + self.b
                low = table[s, 2 * BLK :]
                for g in range(2):
                    at = g * GROUP + e * HALF_BLK
                    rows = slice(at, at + HALF_BLK)
                    self.v[rows, 0:128] = table[s, g * HALF_BLK : (g + 1) * HALF_BLK]
                    self.k[rows, 0:128] = table[s, BLK + g * HALF_BLK : BLK + (g + 1) * HALF_BLK]
                    mask = jnp.where(mine, masks[g], none)
                    both = (low, mask) if g == 0 else (mask, low)
                    self.k[rows, 128:] = jnp.where(left, *both)

        def place_queries(self):
            one_hot = (lax.broadcasted_iota(jnp.int32, (BLK, 128), 0) == lane % BLK).astype(BF)
            for h in range(0, HEADS, 2):
                t0, t1, t2 = (
                    q_ref[self.rows, h * DK + i * 128 : h * DK + (i + 1) * 128] for i in range(3)
                )
                r1, r2 = swap(t1), swap(t2)
                for k, (high, low, swapped) in enumerate(
                    ((t0, t1, r1), (jnp.where(first, r1, r2), r2, t2))
                ):
                    rows = slice((h + k) * BLK, (h + k + 1) * BLK)
                    for g in range(2):
                        self.q[g, rows, 0:128] = high
                    self.q[0, rows, 128:] = jnp.where(first, low, one_hot)
                    self.q[1, rows, 128:] = jnp.where(first, one_hot, swapped)

        def score(self):
            self.top = None
            for g, rows in enumerate(groups):
                s = dot(self.k[rows, :], self.q[g], 1, 1)
                self.p[rows, :] = s
                m = jnp.max(s, axis=0, keepdims=True)
                self.top = m if self.top is None else jnp.maximum(self.top, m)

        def weigh(self):
            self.out_t = None
            for rows in groups:
                p = jnp.exp2((self.p[rows, :] - self.top) * (scale * LOG2E))
                self.p[rows, :] = p
                pb = p.astype(BF)
                self.pb[rows, :] = pb
                o = dot(self.v[rows, : DV + 16], pb, 0, 0)
                self.out_t = o if self.out_t is None else self.out_t + o

        def output(self):
            out = jnp.transpose(self.out_t)
            inverse = 1.0 / out[:, 128:129]
            att = (out[:, :128] * inverse).astype(BF)
            for h in range(HEADS):
                rows = slice(h * BLK, (h + 1) * BLK)
                cols = slice(h * DV, (h + 1) * DV)
                att_ref[self.rows, cols] = att[rows]
                do = (do_ref[self.rows, cols].astype(F32) * inverse[rows]).astype(BF)
                delta = jnp.sum(do.astype(F32) * att[rows].astype(F32), axis=1, keepdims=True)
                delta = jnp.broadcast_to(-delta, (BLK, 128))
                high = delta.astype(BF).astype(F32)
                rest = delta - high
                mid = rest.astype(BF).astype(F32)
                extra = jnp.where(
                    lane == 0, high, jnp.where(lane == 1, mid, jnp.where(lane == 2, rest - mid, 0.0))
                )
                self.do[rows, 0:128] = do
                self.do[rows, 128:] = extra.astype(BF)

        def backward(self):
            do_all = self.do[...]
            self.dq_t = []
            for g, rows in enumerate(groups):
                dp = dot(self.v[rows, :], do_all, 1, 1)
                ds = (self.p[rows, :] * dp).astype(BF)
                self.dv[rows, :] = dot(self.pb[rows, :], self.do[:, 0:128], 1, 0)
                self.dk[rows, :] = dot(ds, self.q[g], 1, 0) * scale
                self.dq_t.append(dot(self.k[rows, :], ds, 0, 0))

        def packed(self, e):
            r1 = slice(e * HALF_BLK, (e + 1) * HALF_BLK)
            r2 = slice(GROUP + e * HALF_BLK, GROUP + (e + 1) * HALF_BLK)
            return (
                (slice(0, HALF_BLK), self.dv[r1, :]),
                (slice(HALF_BLK, BLK), self.dv[r2, :]),
                (slice(BLK, BLK + HALF_BLK), self.dk[r1, 0:128]),
                (slice(BLK + HALF_BLK, 2 * BLK), self.dk[r2, 0:128]),
                (slice(2 * BLK, ROWS), jnp.where(left, self.dk[r1, 128:], self.dk[r2, 128:])),
            )

        def store_parts(self):
            for e in range(SEL):
                at = jnp.minimum(src_ref[self.b, e], n_remote)
                for rows, x in self.packed(e):
                    part[at, rows] = x.astype(BF)

        def add_own(self):
            for rows, x in self.packed(0):
                own_ref[self.b, rows] += x
            for e in range(1, SEL):
                s = src_ref[self.b, e]

                @pl.when(s >= n_remote)
                def _():
                    for rows, x in self.packed(e):
                        own_ref[s - n_remote, rows] += x

        def query_grads(self):
            high = jnp.transpose(self.dq_t[0][:128] + self.dq_t[1][:128]) * scale
            low = self.dq_t[0][128:192] + self.dq_t[1][192:]
            low = jnp.transpose(jnp.concatenate([low, low], axis=0)) * scale
            for h in range(0, HEADS, 2):
                even, odd = slice(h * BLK, (h + 1) * BLK), slice((h + 1) * BLK, (h + 2) * BLK)
                turned = swap(high[odd])
                parts = (
                    high[even],
                    jnp.where(first, low[even], turned),
                    jnp.where(first, turned, low[odd]),
                )
                for i, x in enumerate(parts):
                    dq_ref[self.rows, h * DK + i * 128 : h * DK + (i + 1) * 128] = x.astype(BF)

    blocks = [Block(i) for i in range(PAIR)]
    for block in blocks:
        block.place_queries()

    @pl.when(step == 0)
    def _():
        for load in loads:
            load.wait()

    blocks[0].place_keys()
    blocks[1].place_keys()
    blocks[0].score()
    blocks[2].place_keys()
    blocks[1].score()
    blocks[0].weigh()
    blocks[3].place_keys()
    blocks[2].score()
    blocks[1].weigh()
    blocks[0].output()
    blocks[3].score()
    blocks[2].weigh()
    blocks[1].output()
    blocks[0].backward()
    blocks[3].weigh()
    blocks[2].output()
    blocks[1].backward()
    blocks[0].store_parts()
    blocks[3].output()
    blocks[2].backward()
    blocks[1].store_parts()
    blocks[3].backward()
    blocks[2].store_parts()
    blocks[3].store_parts()
    last = step == LOCAL // PAIR - 1

    @pl.when(last)
    def _():
        for store in stores:
            store.start()

    for block in blocks:
        block.query_grads()
    for block in blocks:
        block.add_own()

    @pl.when(last)
    def _():
        for store in stores:
            store.wait()


def attend(src, queries, d_out, local, near, far):
    tokens = LOCAL * BLK
    keys = SEL * BLK
    rows = HEADS * BLK
    n_near, n_far = (x.shape[0] * x.shape[1] for x in (near, far))
    anywhere = pl.BlockSpec(memory_space=pl.ANY)
    plane = near.shape[0]
    return pl.pallas_call(
        attend_kernel,
        grid_spec=pltpu.PrefetchScalarGridSpec(
            num_scalar_prefetch=1,
            grid=(LOCAL // PAIR,),
            in_specs=[
                pl.BlockSpec((PAIR * BLK, HEADS * DK), lambda b, src: (b, 0)),
                pl.BlockSpec((PAIR * BLK, HEADS * DV), lambda b, src: (b, 0)),
                anywhere,
                anywhere,
                anywhere,
            ],
            out_specs=[
                pl.BlockSpec((PAIR * BLK, HEADS * DV), lambda b, src: (b, 0)),
                pl.BlockSpec((PAIR * BLK, HEADS * DK), lambda b, src: (b, 0)),
                anywhere,
                anywhere,
                anywhere,
                pl.BlockSpec((LOCAL, ROWS, 128), lambda b, src: (0, 0, 0)),
            ],
            scratch_shapes=[
                pltpu.VMEM((n_near + n_far + LOCAL, ROWS, 128), BF),
                pltpu.VMEM((n_near + n_far + 1, ROWS, 128), BF),
                pltpu.VMEM((PAIR, keys, 256), BF),
                pltpu.VMEM((PAIR, keys, 256), BF),
                pltpu.VMEM((PAIR, 2, rows, 256), BF),
                pltpu.VMEM((PAIR, rows, 256), BF),
                pltpu.VMEM((PAIR, keys, rows), F32),
                pltpu.VMEM((PAIR, keys, rows), BF),
                pltpu.VMEM((PAIR, keys, 256), F32),
                pltpu.VMEM((PAIR, keys, 128), F32),
                pltpu.SemaphoreType.DMA((5,)),
            ],
        ),
        out_shape=(
            jax.ShapeDtypeStruct((tokens, HEADS * DV), BF),
            jax.ShapeDtypeStruct((tokens, HEADS * DK), BF),
            jax.ShapeDtypeStruct((plane, ROWS, 128), BF),
            jax.ShapeDtypeStruct((plane, 2, ROWS, 128), BF),
            jax.ShapeDtypeStruct((n_far, ROWS, 128), BF),
            jax.ShapeDtypeStruct((LOCAL, ROWS, 128), F32),
        ),
        compiler_params=params(),
        name="attend",
    )(
        src,
        queries,
        d_out,
        local,
        near,
        far.reshape(n_far, ROWS, 128),
    )


def shards(depth, plane, queries, keys, values, selected, d_out):
    me = lax.axis_index(("z", "y", "x"))
    z = lax.axis_index("z")
    seq_count = depth * plane
    per_half = LOCAL // 2
    half_index = selected // per_half
    is_late = half_index >= seq_count
    owners = jnp.where(is_late, 2 * seq_count - 1 - half_index, half_index)
    inner = selected % per_half + jnp.where(is_late, per_half, 0)
    remote = owners != me
    offset = (owners // plane - z + depth) % depth
    order = jnp.where(offset < 2, offset, jnp.where(offset == depth - 1, 2, offset + 1))
    in_plane = owners % plane
    slots = jnp.where(
        order < 3, order * plane + in_plane, 3 * plane + in_plane * (depth - 3) + order - 3
    )
    src = jnp.where(remote, slots, seq_count + inner).astype(jnp.int32)
    flat = jnp.where(remote, in_plane * depth + order, -1).reshape(-1)
    hits = flat[:, None] == jnp.arange(seq_count, dtype=jnp.int32)[None, :]
    wanted = jnp.max(jnp.where(hits, inner.reshape(-1)[:, None] + 1, 0), axis=0)
    exchange = functools.partial(
        lax.all_to_all, axis_name=("y", "x"), split_axis=0, concat_axis=0, tiled=True
    )
    up = [(i, (i + 1) % depth) for i in range(depth)]
    down = [(i, (i - 1) % depth) for i in range(depth)]
    where_z = z.reshape(1).astype(jnp.int32)

    local = pack(keys.T, values)
    above = lax.ppermute(local, "z", down)
    below = lax.ppermute(local, "z", up)
    asked = exchange(wanted.reshape(plane, 1, depth)).reshape(plane, depth)
    column = lax.all_gather(local, "z")
    near = exchange(build(0, 3, where_z, asked, local, above, below))
    far = exchange(build(3, depth - 3, where_z, asked, column))
    attended, d_queries, part_here, part_side, part_far, own = attend(
        src, queries, d_out, local, near, far
    )
    far_sums = sum_far(depth, where_z, asked, exchange(part_far.reshape(far.shape)))
    far_sums, part_side = lax.optimization_barrier((far_sums, part_side))
    mine = lax.psum_scatter(far_sums, "z", scatter_dimension=0)
    to_above, to_below = sum_near(1, asked, exchange(part_side))
    to_above, to_below, part_here = lax.optimization_barrier((to_above, to_below, part_here))
    from_below = lax.ppermute(to_above, "z", up)
    from_above = lax.ppermute(to_below, "z", down)
    (here,) = sum_near(0, asked, exchange(part_here[:, None]))
    d_keys_t, d_values = finish(own, here, from_below, from_above, mine)
    return attended, d_queries, d_keys_t.T, d_values


def solution(mesh):
    grid = Mesh(mesh.devices.reshape(SIDES + (-1,)), ("z", "y", "x", "grp"))
    spec = P(("z", "y", "x"), "grp")
    return jax.shard_map(
        functools.partial(shards, SIDES[0], SIDES[1] * SIDES[2]),
        mesh=grid,
        in_specs=(spec,) * 5,
        out_specs=(spec,) * 4,
        check_vma=False,
    )
```

```python
import functools

import jax
import jax.numpy as jnp
from jax import lax
from jax.experimental import pallas as pl
from jax.experimental.pallas import tpu as pltpu
from jax.sharding import Mesh, PartitionSpec as P

BLK = 64
SEL = 16
HEADS = 8
DK = 192
DV = 128
ROWS = 160
SIDES = (8, 4, 4)
LOCAL = 8
LOG2E = 1.4426950408889634
NEG = -1e30
BF = jnp.bfloat16
F32 = jnp.float32


def params(mib=56):
    return pltpu.CompilerParams(vmem_limit_bytes=mib * 1024 * 1024)


def pack_kernel(k_ref, v_ref, out_ref):
    for b in range(0, LOCAL, 2):
        pair = jnp.transpose(k_ref[:, b * BLK : (b + 2) * BLK])
        for i in range(2):
            k = pair[i * BLK : (i + 1) * BLK]
            out_ref[b + i, 0:BLK] = v_ref[(b + i) * BLK : (b + i + 1) * BLK, :]
            out_ref[b + i, BLK : 2 * BLK] = k[:, :128]
            low = k[:, 128:]
            out_ref[b + i, 2 * BLK :] = jnp.concatenate([low[:32], low[32:]], axis=1)


def pack(keys_t, values):
    return pl.pallas_call(
        pack_kernel,
        out_shape=jax.ShapeDtypeStruct((LOCAL, ROWS, 128), BF),
        compiler_params=params(),
        name="pack",
    )(keys_t, values)


def build_kernel(first, req_ref, *refs):
    tables, out_hbm = refs[: (len(refs) - 3) // 2], refs[(len(refs) - 3) // 2]
    held, (load_sems, sems) = refs[-2 - len(tables) : -2], refs[-2:]
    plane, count = out_hbm.shape[:2]
    loads = [
        pltpu.make_async_copy(t, h, load_sems.at[i]) for i, (t, h) in enumerate(zip(tables, held))
    ]
    for load in loads:
        load.start()
    sends = []
    for d in range(count):
        loads[d].wait()
        for c in range(plane):
            r = jnp.maximum(req_ref[c, first + d], 1) - 1
            sends.append(pltpu.make_async_copy(held[d].at[r], out_hbm.at[c, d], sems.at[c, d]))
            sends[-1].start()
    for send in sends:
        send.wait()


def build(first, req, *tables):
    plane, count = req.shape[0], len(tables)
    anywhere = pl.BlockSpec(memory_space=pl.ANY)
    return pl.pallas_call(
        functools.partial(build_kernel, first),
        grid_spec=pltpu.PrefetchScalarGridSpec(
            num_scalar_prefetch=1,
            grid=(1,),
            in_specs=[anywhere] * len(tables),
            out_specs=anywhere,
            scratch_shapes=[pltpu.VMEM(t.shape, BF) for t in tables]
            + [pltpu.SemaphoreType.DMA((len(tables),)), pltpu.SemaphoreType.DMA((plane, count))],
        ),
        out_shape=jax.ShapeDtypeStruct((plane, count, ROWS, 128), BF),
        compiler_params=params(),
        name="build",
    )(req, *tables)


def sum_blocks(first, req_ref, ret_hbm, buf, acc, staged, in_sems, out_sems, target):
    plane, count = ret_hbm.shape[:2]
    loads = [
        pltpu.make_async_copy(ret_hbm.at[:, d], buf.at[d], in_sems.at[d]) for d in range(count)
    ]
    for load in loads:
        load.start()
    stores = []
    for d in range(count):
        loads[d].wait()
        acc[...] = jnp.zeros_like(acc)
        for c in range(plane):
            acc[req_ref[c, first + d]] += buf[d, c].astype(F32)
        staged[d] = acc[1:].astype(BF)
        stores.append(pltpu.make_async_copy(staged.at[d], target(d), out_sems.at[d]))
        stores[-1].start()
    return stores


def sum_kernel(first, req_ref, ret_hbm, *refs):
    outs, (buf, acc, staged, in_sems, out_sems) = refs[:-5], refs[-5:]
    for store in sum_blocks(
        first, req_ref, ret_hbm, buf, acc, staged, in_sems, out_sems, lambda d: outs[d]
    ):
        store.wait()


def sum_scratch(plane, count, depth):
    return [
        pltpu.VMEM((count, plane, ROWS, 128), BF),
        pltpu.VMEM((LOCAL + 1, ROWS, 128), F32),
        pltpu.VMEM((count + 1, LOCAL, ROWS, 128), BF),
        pltpu.SemaphoreType.DMA((count,)),
        pltpu.SemaphoreType.DMA((depth,)),
    ]


def sum_returned(first, req, returned):
    plane, count = returned.shape[:2]
    anywhere = pl.BlockSpec(memory_space=pl.ANY)
    return pl.pallas_call(
        functools.partial(sum_kernel, first),
        grid_spec=pltpu.PrefetchScalarGridSpec(
            num_scalar_prefetch=1,
            grid=(1,),
            in_specs=[anywhere],
            out_specs=[anywhere] * count,
            scratch_shapes=sum_scratch(plane, count, count),
        ),
        out_shape=[jax.ShapeDtypeStruct((LOCAL, ROWS, 128), BF)] * count,
        compiler_params=params(),
        name="sum_returned",
    )(req, returned)


def finish_kernel(own_ref, *refs):
    got_refs, (dk_ref, dv_ref) = refs[:-2], refs[-2:]
    for b in range(0, LOCAL, 2):
        pair = []
        for i in range(b, b + 2):
            total = own_ref[i]
            for got_ref in got_refs:
                total = total + got_ref[i].astype(F32)
            dv_ref[i * BLK : (i + 1) * BLK, :] = total[0:BLK].astype(BF)
            low = total[2 * BLK :]
            low = jnp.concatenate([low[:, :64], low[:, 64:]], axis=0)
            pair.append(jnp.concatenate([total[BLK : 2 * BLK], low], axis=1))
        pair = jnp.concatenate(pair, axis=0)
        dk_ref[:, b * BLK : (b + 2) * BLK] = jnp.transpose(pair).astype(BF)


def finish(own, *got):
    return pl.pallas_call(
        finish_kernel,
        out_shape=(
            jax.ShapeDtypeStruct((DK, LOCAL * BLK), BF),
            jax.ShapeDtypeStruct((LOCAL * BLK, DV), BF),
        ),
        compiler_params=params(),
        name="finish",
    )(own, *got)


def dot(a, b, da, db):
    return lax.dot_general(a, b, (((da,), (db,)), ((), ())), preferred_element_type=F32)


def swap(x):
    return jnp.concatenate([x[:, 64:], x[:, :64]], axis=1)


HALF_BLK = BLK // 2
GROUP = SEL * HALF_BLK
PAIR = 4


def lane_ids(rows):
    return lax.broadcasted_iota(jnp.int32, (rows, 128), 1)


def attend_kernel(
    src_ref,
    q_ref,
    do_ref,
    local_hbm,
    near_hbm,
    far_hbm,
    att_ref,
    dq_ref,
    part_here_hbm,
    part_side_hbm,
    part_far_hbm,
    own_ref,
    table,
    part,
    k_bufs,
    v_bufs,
    q_bufs,
    do_bufs,
    p_bufs,
    pb_bufs,
    dk_bufs,
    dv_bufs,
    sems,
):
    step = pl.program_id(0)
    plane, n_far = near_hbm.shape[0], far_hbm.shape[0]
    n_near = plane * near_hbm.shape[1]
    n_remote = n_near + n_far
    scale = DK**-0.5
    left = lane_ids(HALF_BLK) < 64
    lane = lane_ids(BLK)
    first = lane < 64
    groups = [slice(0, GROUP), slice(GROUP, 2 * GROUP)]

    loads = [(near_hbm.at[:, d], d * plane, plane) for d in range(near_hbm.shape[1])]
    loads += [(local_hbm, n_remote, LOCAL), (far_hbm, n_near, n_far)]
    loads = [
        pltpu.make_async_copy(ref, table.at[pl.ds(at, n)], sems.at[i])
        for i, (ref, at, n) in enumerate(loads)
    ]
    stores = [(part_far_hbm, n_near, n_far), (part_here_hbm, 0, plane)]
    stores += [
        (part_side_hbm.at[:, d], (d + 1) * plane, plane) for d in range(part_side_hbm.shape[1])
    ]
    stores = [
        pltpu.make_async_copy(part.at[pl.ds(at, n)], ref, sems.at[i])
        for i, (ref, at, n) in enumerate(stores)
    ]

    @pl.when(step == 0)
    def _():
        for load in loads:
            load.start()
        own_ref[...] = jnp.zeros_like(own_ref)
        for i in range(PAIR):
            v_bufs[i, :, 128:] = jnp.ones((2 * GROUP, 128), BF)

    class Block:
        def __init__(self, i):
            self.i, self.b = i, step * PAIR + i
            self.rows = slice(i * BLK, (i + 1) * BLK)
            self.k, self.v, self.q, self.do = (x.at[i] for x in (k_bufs, v_bufs, q_bufs, do_bufs))
            self.p, self.pb, self.dk, self.dv = (x.at[i] for x in (p_bufs, pb_bufs, dk_bufs, dv_bufs))

        def place_keys(self):
            key_id = lax.broadcasted_iota(jnp.int32, (HALF_BLK, 128), 0)
            query_id = lane_ids(HALF_BLK) % BLK
            none = jnp.zeros((HALF_BLK, 128), BF)
            masks = [
                jnp.where(key_id + g * HALF_BLK > query_id, NEG, 0.0).astype(BF) for g in range(2)
            ]
            for e in range(SEL):
                s = src_ref[self.b, e]
                mine = s == n_remote + self.b
                low = table[s, 2 * BLK :]
                for g in range(2):
                    at = g * GROUP + e * HALF_BLK
                    rows = slice(at, at + HALF_BLK)
                    self.v[rows, 0:128] = table[s, g * HALF_BLK : (g + 1) * HALF_BLK]
                    self.k[rows, 0:128] = table[s, BLK + g * HALF_BLK : BLK + (g + 1) * HALF_BLK]
                    mask = jnp.where(mine, masks[g], none)
                    both = (low, mask) if g == 0 else (mask, low)
                    self.k[rows, 128:] = jnp.where(left, *both)

        def place_queries(self):
            one_hot = (lax.broadcasted_iota(jnp.int32, (BLK, 128), 0) == lane % BLK).astype(BF)
            for h in range(0, HEADS, 2):
                t0, t1, t2 = (
                    q_ref[self.rows, h * DK + i * 128 : h * DK + (i + 1) * 128] for i in range(3)
                )
                r1, r2 = swap(t1), swap(t2)
                for k, (high, low, swapped) in enumerate(
                    ((t0, t1, r1), (jnp.where(first, r1, r2), r2, t2))
                ):
                    rows = slice((h + k) * BLK, (h + k + 1) * BLK)
                    for g in range(2):
                        self.q[g, rows, 0:128] = high
                    self.q[0, rows, 128:] = jnp.where(first, low, one_hot)
                    self.q[1, rows, 128:] = jnp.where(first, one_hot, swapped)

        def score(self):
            self.top = None
            for g, rows in enumerate(groups):
                s = dot(self.k[rows, :], self.q[g], 1, 1)
                self.p[rows, :] = s
                m = jnp.max(s, axis=0, keepdims=True)
                self.top = m if self.top is None else jnp.maximum(self.top, m)

        def weigh(self):
            self.out_t = None
            for rows in groups:
                p = jnp.exp2((self.p[rows, :] - self.top) * (scale * LOG2E))
                self.p[rows, :] = p
                pb = p.astype(BF)
                self.pb[rows, :] = pb
                o = dot(self.v[rows, : DV + 16], pb, 0, 0)
                self.out_t = o if self.out_t is None else self.out_t + o

        def output(self):
            out = jnp.transpose(self.out_t)
            inverse = 1.0 / out[:, 128:129]
            att = (out[:, :128] * inverse).astype(BF)
            for h in range(HEADS):
                rows = slice(h * BLK, (h + 1) * BLK)
                cols = slice(h * DV, (h + 1) * DV)
                att_ref[self.rows, cols] = att[rows]
                do = (do_ref[self.rows, cols].astype(F32) * inverse[rows]).astype(BF)
                delta = jnp.sum(do.astype(F32) * att[rows].astype(F32), axis=1, keepdims=True)
                delta = jnp.broadcast_to(-delta, (BLK, 128))
                high = delta.astype(BF).astype(F32)
                rest = delta - high
                mid = rest.astype(BF).astype(F32)
                extra = jnp.where(
                    lane == 0, high, jnp.where(lane == 1, mid, jnp.where(lane == 2, rest - mid, 0.0))
                )
                self.do[rows, 0:128] = do
                self.do[rows, 128:] = extra.astype(BF)

        def backward(self):
            do_all = self.do[...]
            self.dq_t = []
            for g, rows in enumerate(groups):
                dp = dot(self.v[rows, :], do_all, 1, 1)
                ds = (self.p[rows, :] * dp).astype(BF)
                self.dv[rows, :] = dot(self.pb[rows, :], self.do[:, 0:128], 1, 0)
                self.dk[rows, :] = dot(ds, self.q[g], 1, 0) * scale
                self.dq_t.append(dot(self.k[rows, :], ds, 0, 0))

        def packed(self, e):
            r1 = slice(e * HALF_BLK, (e + 1) * HALF_BLK)
            r2 = slice(GROUP + e * HALF_BLK, GROUP + (e + 1) * HALF_BLK)
            return (
                (slice(0, HALF_BLK), self.dv[r1, :]),
                (slice(HALF_BLK, BLK), self.dv[r2, :]),
                (slice(BLK, BLK + HALF_BLK), self.dk[r1, 0:128]),
                (slice(BLK + HALF_BLK, 2 * BLK), self.dk[r2, 0:128]),
                (slice(2 * BLK, ROWS), jnp.where(left, self.dk[r1, 128:], self.dk[r2, 128:])),
            )

        def store_parts(self):
            for e in range(SEL):
                at = jnp.minimum(src_ref[self.b, e], n_remote)
                for rows, x in self.packed(e):
                    part[at, rows] = x.astype(BF)

        def add_own(self):
            for rows, x in self.packed(0):
                own_ref[self.b, rows] += x
            for e in range(1, SEL):
                s = src_ref[self.b, e]

                @pl.when(s >= n_remote)
                def _():
                    for rows, x in self.packed(e):
                        own_ref[s - n_remote, rows] += x

        def query_grads(self):
            high = jnp.transpose(self.dq_t[0][:128] + self.dq_t[1][:128]) * scale
            low = self.dq_t[0][128:192] + self.dq_t[1][192:]
            low = jnp.transpose(jnp.concatenate([low, low], axis=0)) * scale
            for h in range(0, HEADS, 2):
                even, odd = slice(h * BLK, (h + 1) * BLK), slice((h + 1) * BLK, (h + 2) * BLK)
                turned = swap(high[odd])
                parts = (
                    high[even],
                    jnp.where(first, low[even], turned),
                    jnp.where(first, turned, low[odd]),
                )
                for i, x in enumerate(parts):
                    dq_ref[self.rows, h * DK + i * 128 : h * DK + (i + 1) * 128] = x.astype(BF)

    blocks = [Block(i) for i in range(PAIR)]
    for block in blocks:
        block.place_queries()

    @pl.when(step == 0)
    def _():
        for load in loads:
            load.wait()

    blocks[0].place_keys()
    blocks[1].place_keys()
    blocks[0].score()
    blocks[2].place_keys()
    blocks[1].score()
    blocks[0].weigh()
    blocks[3].place_keys()
    blocks[2].score()
    blocks[1].weigh()
    blocks[0].output()
    blocks[3].score()
    blocks[2].weigh()
    blocks[1].output()
    blocks[0].backward()
    blocks[3].weigh()
    blocks[2].output()
    blocks[1].backward()
    blocks[0].store_parts()
    blocks[3].output()
    blocks[2].backward()
    blocks[1].store_parts()
    blocks[3].backward()
    blocks[2].store_parts()
    blocks[3].store_parts()
    last = step == LOCAL // PAIR - 1

    @pl.when(last)
    def _():
        for store in stores:
            store.start()

    for block in blocks:
        block.query_grads()
    for block in blocks:
        block.add_own()

    @pl.when(last)
    def _():
        for store in stores:
            store.wait()


def attend(src, queries, d_out, local, near, far):
    tokens = LOCAL * BLK
    keys = SEL * BLK
    rows = HEADS * BLK
    n_near, n_far = (x.shape[0] * x.shape[1] for x in (near, far))
    anywhere = pl.BlockSpec(memory_space=pl.ANY)
    plane = near.shape[0]
    return pl.pallas_call(
        attend_kernel,
        grid_spec=pltpu.PrefetchScalarGridSpec(
            num_scalar_prefetch=1,
            grid=(LOCAL // PAIR,),
            in_specs=[
                pl.BlockSpec((PAIR * BLK, HEADS * DK), lambda b, src: (b, 0)),
                pl.BlockSpec((PAIR * BLK, HEADS * DV), lambda b, src: (b, 0)),
                anywhere,
                anywhere,
                anywhere,
            ],
            out_specs=[
                pl.BlockSpec((PAIR * BLK, HEADS * DV), lambda b, src: (b, 0)),
                pl.BlockSpec((PAIR * BLK, HEADS * DK), lambda b, src: (b, 0)),
                anywhere,
                anywhere,
                anywhere,
                pl.BlockSpec((LOCAL, ROWS, 128), lambda b, src: (0, 0, 0)),
            ],
            scratch_shapes=[
                pltpu.VMEM((n_near + n_far + LOCAL, ROWS, 128), BF),
                pltpu.VMEM((n_near + n_far + 1, ROWS, 128), BF),
                pltpu.VMEM((PAIR, keys, 256), BF),
                pltpu.VMEM((PAIR, keys, 256), BF),
                pltpu.VMEM((PAIR, 2, rows, 256), BF),
                pltpu.VMEM((PAIR, rows, 256), BF),
                pltpu.VMEM((PAIR, keys, rows), F32),
                pltpu.VMEM((PAIR, keys, rows), BF),
                pltpu.VMEM((PAIR, keys, 256), F32),
                pltpu.VMEM((PAIR, keys, 128), F32),
                pltpu.SemaphoreType.DMA((5,)),
            ],
        ),
        out_shape=(
            jax.ShapeDtypeStruct((tokens, HEADS * DV), BF),
            jax.ShapeDtypeStruct((tokens, HEADS * DK), BF),
            jax.ShapeDtypeStruct((plane, ROWS, 128), BF),
            jax.ShapeDtypeStruct((plane, 2, ROWS, 128), BF),
            jax.ShapeDtypeStruct((n_far, ROWS, 128), BF),
            jax.ShapeDtypeStruct((LOCAL, ROWS, 128), F32),
        ),
        compiler_params=params(),
        name="attend",
    )(
        src,
        queries,
        d_out,
        local,
        near,
        far.reshape(n_far, ROWS, 128),
    )


def pass_on(terms, perm):
    total = lax.ppermute(terms[0], "z", perm)
    for term in terms[1:]:
        total = (total.astype(F32) + term.astype(F32)).astype(BF)
        total = lax.ppermute(total, "z", perm)
    return total


def shards(depth, plane, queries, keys, values, selected, d_out):
    me = lax.axis_index(("z", "y", "x"))
    z = lax.axis_index("z")
    seq_count = depth * plane
    per_half = LOCAL // 2
    half_index = selected // per_half
    is_late = half_index >= seq_count
    owners = jnp.where(is_late, 2 * seq_count - 1 - half_index, half_index)
    inner = selected % per_half + jnp.where(is_late, per_half, 0)
    remote = owners != me
    offset = (owners // plane - z + depth) % depth
    order = jnp.where(offset < 2, offset, jnp.where(offset == depth - 1, 2, offset + 1))
    in_plane = owners % plane
    slots = jnp.where(
        order < 3, order * plane + in_plane, 3 * plane + in_plane * (depth - 3) + order - 3
    )
    src = jnp.where(remote, slots, seq_count + inner).astype(jnp.int32)
    flat = jnp.where(remote, in_plane * depth + order, -1).reshape(-1)
    hits = flat[:, None] == jnp.arange(seq_count, dtype=jnp.int32)[None, :]
    wanted = jnp.max(jnp.where(hits, inner.reshape(-1)[:, None] + 1, 0), axis=0)
    exchange = functools.partial(
        lax.all_to_all, axis_name=("y", "x"), split_axis=0, concat_axis=0, tiled=True
    )
    up = [(i, (i + 1) % depth) for i in range(depth)]
    down = [(i, (i - 1) % depth) for i in range(depth)]

    local = pack(keys.T, values)
    above, below = [local], [local]
    for _ in range(depth // 2):
        above.append(lax.ppermute(above[-1], "z", down))
    for _ in range(depth - 1 - depth // 2):
        below.append(lax.ppermute(below[-1], "z", up))
    asked = exchange(wanted.reshape(plane, 1, depth)).reshape(plane, depth)
    near = exchange(build(0, asked, local, above[1], below[1]))
    far = exchange(build(3, asked, *above[2:], *below[:1:-1]))
    attended, d_queries, part_here, part_side, part_far, own = attend(
        src, queries, d_out, local, near, far
    )
    far_sums = sum_returned(3, asked, exchange(part_far.reshape(far.shape)))
    *far_sums, part_side = lax.optimization_barrier((*far_sums, part_side))
    n_above = depth // 2 - 1
    to_above, to_below = far_sums[:n_above][::-1], far_sums[n_above:]
    side_above, side_below = sum_returned(1, asked, exchange(part_side))
    *sides, part_here = lax.optimization_barrier((side_above, side_below, part_here))
    rising = pass_on(to_above + sides[:1], up)
    falling = pass_on(to_below + sides[1:], down)
    (here,) = sum_returned(0, asked, exchange(part_here[:, None]))
    d_keys_t, d_values = finish(own, here, rising, falling)
    return attended, d_queries, d_keys_t.T, d_values


def solution(mesh):
    grid = Mesh(mesh.devices.reshape(SIDES + (-1,)), ("z", "y", "x", "grp"))
    spec = P(("z", "y", "x"), "grp")
    return jax.shard_map(
        functools.partial(shards, SIDES[0], SIDES[1] * SIDES[2]),
        mesh=grid,
        in_specs=(spec,) * 5,
        out_specs=(spec,) * 4,
        check_vma=False,
    )
```

```python
import functools

import jax
import jax.numpy as jnp
from jax import lax
from jax.experimental import pallas as pl
from jax.experimental.pallas import tpu as pltpu
from jax.sharding import Mesh, PartitionSpec as P

BLK = 64
SEL = 16
HEADS = 8
DK = 192
DV = 128
ROWS = 160
SIDES = (8, 4, 4)
LOCAL = 8
LOG2E = 1.4426950408889634
NEG = -1e30
BF = jnp.bfloat16
F32 = jnp.float32


def params(mib=56):
    return pltpu.CompilerParams(vmem_limit_bytes=mib * 1024 * 1024)


def pack_kernel(k_ref, v_ref, out_ref):
    for b in range(0, LOCAL, 2):
        pair = jnp.transpose(k_ref[:, b * BLK : (b + 2) * BLK])
        for i in range(2):
            k = pair[i * BLK : (i + 1) * BLK]
            out_ref[b + i, 0:BLK] = v_ref[(b + i) * BLK : (b + i + 1) * BLK, :]
            out_ref[b + i, BLK : 2 * BLK] = k[:, :128]
            low = k[:, 128:]
            out_ref[b + i, 2 * BLK :] = jnp.concatenate([low[:32], low[32:]], axis=1)


def pack(keys_t, values):
    return pl.pallas_call(
        pack_kernel,
        out_shape=jax.ShapeDtypeStruct((LOCAL, ROWS, 128), BF),
        compiler_params=params(16),
        name="pack",
    )(keys_t, values)


def build_kernel(first, req_ref, *refs):
    tables, out_hbm = refs[: (len(refs) - 3) // 2], refs[(len(refs) - 3) // 2]
    held, (load_sems, sems) = refs[-2 - len(tables) : -2], refs[-2:]
    plane, count = out_hbm.shape[:2]
    loads = [
        pltpu.make_async_copy(t, h, load_sems.at[i]) for i, (t, h) in enumerate(zip(tables, held))
    ]
    for load in loads:
        load.start()
    sends = []
    for d in range(count):
        loads[d].wait()
        for c in range(plane):
            r = jnp.maximum(req_ref[c, first + d], 1) - 1
            sends.append(pltpu.make_async_copy(held[d].at[r], out_hbm.at[c, d], sems.at[c, d]))
            sends[-1].start()
    for send in sends:
        send.wait()


def build(first, mib, req, *tables):
    plane, count = req.shape[0], len(tables)
    anywhere = pl.BlockSpec(memory_space=pl.ANY)
    return pl.pallas_call(
        functools.partial(build_kernel, first),
        grid_spec=pltpu.PrefetchScalarGridSpec(
            num_scalar_prefetch=1,
            grid=(1,),
            in_specs=[anywhere] * len(tables),
            out_specs=anywhere,
            scratch_shapes=[pltpu.VMEM(t.shape, BF) for t in tables]
            + [pltpu.SemaphoreType.DMA((len(tables),)), pltpu.SemaphoreType.DMA((plane, count))],
        ),
        out_shape=jax.ShapeDtypeStruct((plane, count, ROWS, 128), BF),
        compiler_params=params(mib),
        name="build",
    )(req, *tables)


def sum_blocks(first, req_ref, ret_hbm, buf, acc, staged, in_sems, out_sems, target):
    plane, count = ret_hbm.shape[:2]
    loads = [
        pltpu.make_async_copy(ret_hbm.at[:, d], buf.at[d], in_sems.at[d]) for d in range(count)
    ]
    for load in loads:
        load.start()
    stores = []
    for d in range(count):
        loads[d].wait()
        acc[...] = jnp.zeros_like(acc)
        for c in range(plane):
            acc[req_ref[c, first + d]] += buf[d, c].astype(F32)
        staged[d] = acc[1:].astype(BF)
        stores.append(pltpu.make_async_copy(staged.at[d], target(d), out_sems.at[d]))
        stores[-1].start()
    return stores


def sum_kernel(first, req_ref, ret_hbm, *refs):
    outs, (buf, acc, staged, in_sems, out_sems) = refs[:-5], refs[-5:]
    for store in sum_blocks(
        first, req_ref, ret_hbm, buf, acc, staged, in_sems, out_sems, lambda d: outs[d]
    ):
        store.wait()


def sum_scratch(plane, count, depth):
    return [
        pltpu.VMEM((count, plane, ROWS, 128), BF),
        pltpu.VMEM((LOCAL + 1, ROWS, 128), F32),
        pltpu.VMEM((count + 1, LOCAL, ROWS, 128), BF),
        pltpu.SemaphoreType.DMA((count,)),
        pltpu.SemaphoreType.DMA((depth,)),
    ]


def sum_returned(first, req, returned):
    plane, count = returned.shape[:2]
    anywhere = pl.BlockSpec(memory_space=pl.ANY)
    return pl.pallas_call(
        functools.partial(sum_kernel, first),
        grid_spec=pltpu.PrefetchScalarGridSpec(
            num_scalar_prefetch=1,
            grid=(1,),
            in_specs=[anywhere],
            out_specs=[anywhere] * count,
            scratch_shapes=sum_scratch(plane, count, count),
        ),
        out_shape=[jax.ShapeDtypeStruct((LOCAL, ROWS, 128), BF)] * count,
        compiler_params=params(16),
        name="sum_returned",
    )(req, returned)


def finish_kernel(req_ref, own_ref, ret_ref, rising_ref, falling_ref, dk_ref, dv_ref, acc):
    acc[1:] = own_ref[...] + rising_ref[...].astype(F32) + falling_ref[...].astype(F32)
    for c in range(ret_ref.shape[0]):
        acc[req_ref[c, 0]] += ret_ref[c, 0].astype(F32)
    for b in range(0, LOCAL, 2):
        pair = []
        for i in range(b, b + 2):
            total = acc[i + 1]
            dv_ref[i * BLK : (i + 1) * BLK, :] = total[0:BLK].astype(BF)
            low = total[2 * BLK :]
            low = jnp.concatenate([low[:, :64], low[:, 64:]], axis=0)
            pair.append(jnp.concatenate([total[BLK : 2 * BLK], low], axis=1))
        pair = jnp.concatenate(pair, axis=0)
        dk_ref[:, b * BLK : (b + 2) * BLK] = jnp.transpose(pair).astype(BF)


def finish(req, own, returned, rising, falling):
    def whole(dims):
        return pl.BlockSpec(dims, lambda i, req: (0,) * len(dims))

    outs = ((DK, LOCAL * BLK), (LOCAL * BLK, DV))
    return pl.pallas_call(
        finish_kernel,
        grid_spec=pltpu.PrefetchScalarGridSpec(
            num_scalar_prefetch=1,
            grid=(1,),
            in_specs=[whole(x.shape) for x in (own, returned, rising, falling)],
            out_specs=[whole(dims) for dims in outs],
            scratch_shapes=[pltpu.VMEM((LOCAL + 1, ROWS, 128), F32)],
        ),
        out_shape=[jax.ShapeDtypeStruct(dims, BF) for dims in outs],
        compiler_params=params(16),
        name="finish",
    )(req, own, returned, rising, falling)


def dot(a, b, da, db):
    return lax.dot_general(a, b, (((da,), (db,)), ((), ())), preferred_element_type=F32)


def swap(x):
    return jnp.concatenate([x[:, 64:], x[:, :64]], axis=1)


HALF_BLK = BLK // 2
GROUP = SEL * HALF_BLK
PAIR = 4


def lane_ids(rows):
    return lax.broadcasted_iota(jnp.int32, (rows, 128), 1)


def attend_kernel(
    src_ref,
    q_ref,
    do_ref,
    local_hbm,
    near_hbm,
    far_hbm,
    att_ref,
    dq_ref,
    part_here_hbm,
    part_side_hbm,
    part_far_hbm,
    own_ref,
    table,
    part,
    k_bufs,
    v_bufs,
    q_bufs,
    do_bufs,
    p_bufs,
    pb_bufs,
    dk_bufs,
    dv_bufs,
    sems,
):
    step = pl.program_id(0)
    plane, n_far = near_hbm.shape[0], far_hbm.shape[0]
    n_near = plane * near_hbm.shape[1]
    n_remote = n_near + n_far
    scale = DK**-0.5
    left = lane_ids(HALF_BLK) < 64
    lane = lane_ids(BLK)
    first = lane < 64
    groups = [slice(0, GROUP), slice(GROUP, 2 * GROUP)]

    loads = [(near_hbm.at[:, d], d * plane, plane) for d in range(near_hbm.shape[1])]
    loads += [(local_hbm, n_remote, LOCAL), (far_hbm, n_near, n_far)]
    loads = [
        pltpu.make_async_copy(ref, table.at[pl.ds(at, n)], sems.at[i])
        for i, (ref, at, n) in enumerate(loads)
    ]
    stores = [(part_far_hbm, n_near, n_far), (part_here_hbm, 0, plane)]
    stores += [
        (part_side_hbm.at[:, d], (d + 1) * plane, plane) for d in range(part_side_hbm.shape[1])
    ]
    stores = [
        pltpu.make_async_copy(part.at[pl.ds(at, n)], ref, sems.at[i])
        for i, (ref, at, n) in enumerate(stores)
    ]

    @pl.when(step == 0)
    def _():
        for load in loads:
            load.start()
        own_ref[...] = jnp.zeros_like(own_ref)
        for i in range(PAIR):
            v_bufs[i, :, 128:] = jnp.ones((2 * GROUP, 128), BF)

    class Block:
        def __init__(self, i):
            self.i, self.b = i, step * PAIR + i
            self.rows = slice(i * BLK, (i + 1) * BLK)
            self.k, self.v, self.q, self.do = (x.at[i] for x in (k_bufs, v_bufs, q_bufs, do_bufs))
            self.p, self.pb, self.dk, self.dv = (x.at[i] for x in (p_bufs, pb_bufs, dk_bufs, dv_bufs))

        def place_keys(self):
            key_id = lax.broadcasted_iota(jnp.int32, (HALF_BLK, 128), 0)
            query_id = lane_ids(HALF_BLK) % BLK
            none = jnp.zeros((HALF_BLK, 128), BF)
            masks = [
                jnp.where(key_id + g * HALF_BLK > query_id, NEG, 0.0).astype(BF) for g in range(2)
            ]
            for e in range(SEL):
                s = src_ref[self.b, e]
                mine = s == n_remote + self.b
                low = table[s, 2 * BLK :]
                for g in range(2):
                    at = g * GROUP + e * HALF_BLK
                    rows = slice(at, at + HALF_BLK)
                    self.v[rows, 0:128] = table[s, g * HALF_BLK : (g + 1) * HALF_BLK]
                    self.k[rows, 0:128] = table[s, BLK + g * HALF_BLK : BLK + (g + 1) * HALF_BLK]
                    mask = jnp.where(mine, masks[g], none)
                    both = (low, mask) if g == 0 else (mask, low)
                    self.k[rows, 128:] = jnp.where(left, *both)

        def place_queries(self):
            one_hot = (lax.broadcasted_iota(jnp.int32, (BLK, 128), 0) == lane % BLK).astype(BF)
            for h in range(0, HEADS, 2):
                t0, t1, t2 = (
                    q_ref[self.rows, h * DK + i * 128 : h * DK + (i + 1) * 128] for i in range(3)
                )
                r1, r2 = swap(t1), swap(t2)
                for k, (high, low, swapped) in enumerate(
                    ((t0, t1, r1), (jnp.where(first, r1, r2), r2, t2))
                ):
                    rows = slice((h + k) * BLK, (h + k + 1) * BLK)
                    for g in range(2):
                        self.q[g, rows, 0:128] = high
                    self.q[0, rows, 128:] = jnp.where(first, low, one_hot)
                    self.q[1, rows, 128:] = jnp.where(first, one_hot, swapped)

        def score(self):
            self.top = None
            for g, rows in enumerate(groups):
                s = dot(self.k[rows, :], self.q[g], 1, 1)
                self.p[rows, :] = s
                m = jnp.max(s, axis=0, keepdims=True)
                self.top = m if self.top is None else jnp.maximum(self.top, m)

        def weigh(self):
            self.out_t = None
            for rows in groups:
                p = jnp.exp2((self.p[rows, :] - self.top) * (scale * LOG2E))
                self.p[rows, :] = p
                pb = p.astype(BF)
                self.pb[rows, :] = pb
                o = dot(self.v[rows, : DV + 16], pb, 0, 0)
                self.out_t = o if self.out_t is None else self.out_t + o

        def output(self):
            out = jnp.transpose(self.out_t)
            inverse = 1.0 / out[:, 128:129]
            att = (out[:, :128] * inverse).astype(BF)
            for h in range(HEADS):
                rows = slice(h * BLK, (h + 1) * BLK)
                cols = slice(h * DV, (h + 1) * DV)
                att_ref[self.rows, cols] = att[rows]
                do = (do_ref[self.rows, cols].astype(F32) * inverse[rows]).astype(BF)
                delta = jnp.sum(do.astype(F32) * att[rows].astype(F32), axis=1, keepdims=True)
                delta = jnp.broadcast_to(-delta, (BLK, 128))
                high = delta.astype(BF).astype(F32)
                rest = delta - high
                mid = rest.astype(BF).astype(F32)
                extra = jnp.where(
                    lane == 0, high, jnp.where(lane == 1, mid, jnp.where(lane == 2, rest - mid, 0.0))
                )
                self.do[rows, 0:128] = do
                self.do[rows, 128:] = extra.astype(BF)

        def backward(self):
            do_all = self.do[...]
            self.dq_t = []
            for g, rows in enumerate(groups):
                dp = dot(self.v[rows, :], do_all, 1, 1)
                ds = (self.p[rows, :] * dp).astype(BF)
                self.dv[rows, :] = dot(self.pb[rows, :], self.do[:, 0:128], 1, 0)
                self.dk[rows, :] = dot(ds, self.q[g], 1, 0) * scale
                self.dq_t.append(dot(self.k[rows, :], ds, 0, 0))

        def packed(self, e):
            r1 = slice(e * HALF_BLK, (e + 1) * HALF_BLK)
            r2 = slice(GROUP + e * HALF_BLK, GROUP + (e + 1) * HALF_BLK)
            return (
                (slice(0, HALF_BLK), self.dv[r1, :]),
                (slice(HALF_BLK, BLK), self.dv[r2, :]),
                (slice(BLK, BLK + HALF_BLK), self.dk[r1, 0:128]),
                (slice(BLK + HALF_BLK, 2 * BLK), self.dk[r2, 0:128]),
                (slice(2 * BLK, ROWS), jnp.where(left, self.dk[r1, 128:], self.dk[r2, 128:])),
            )

        def store_parts(self):
            for e in range(SEL):
                at = jnp.minimum(src_ref[self.b, e], n_remote)
                for rows, x in self.packed(e):
                    part[at, rows] = x.astype(BF)

        def add_own(self):
            for rows, x in self.packed(0):
                own_ref[self.b, rows] += x
            for e in range(1, SEL):
                s = src_ref[self.b, e]

                @pl.when(s >= n_remote)
                def _():
                    for rows, x in self.packed(e):
                        own_ref[s - n_remote, rows] += x

        def query_grads(self):
            high = jnp.transpose(self.dq_t[0][:128] + self.dq_t[1][:128]) * scale
            low = self.dq_t[0][128:192] + self.dq_t[1][192:]
            low = jnp.transpose(jnp.concatenate([low, low], axis=0)) * scale
            for h in range(0, HEADS, 2):
                even, odd = slice(h * BLK, (h + 1) * BLK), slice((h + 1) * BLK, (h + 2) * BLK)
                turned = swap(high[odd])
                parts = (
                    high[even],
                    jnp.where(first, low[even], turned),
                    jnp.where(first, turned, low[odd]),
                )
                for i, x in enumerate(parts):
                    dq_ref[self.rows, h * DK + i * 128 : h * DK + (i + 1) * 128] = x.astype(BF)

    blocks = [Block(i) for i in range(PAIR)]
    for block in blocks:
        block.place_queries()

    @pl.when(step == 0)
    def _():
        for load in loads:
            load.wait()

    blocks[0].place_keys()
    blocks[1].place_keys()
    blocks[0].score()
    blocks[2].place_keys()
    blocks[1].score()
    blocks[0].weigh()
    blocks[3].place_keys()
    blocks[2].score()
    blocks[1].weigh()
    blocks[0].output()
    blocks[3].score()
    blocks[2].weigh()
    blocks[1].output()
    blocks[0].backward()
    blocks[3].weigh()
    blocks[2].output()
    blocks[1].backward()
    blocks[0].store_parts()
    blocks[3].output()
    blocks[2].backward()
    blocks[1].store_parts()
    blocks[3].backward()
    blocks[2].store_parts()
    blocks[3].store_parts()
    last = step == LOCAL // PAIR - 1

    @pl.when(last)
    def _():
        for store in stores:
            store.start()

    for block in blocks:
        block.query_grads()
    for block in blocks:
        block.add_own()

    @pl.when(last)
    def _():
        for store in stores:
            store.wait()


def attend(src, queries, d_out, local, near, far):
    tokens = LOCAL * BLK
    keys = SEL * BLK
    rows = HEADS * BLK
    n_near, n_far = (x.shape[0] * x.shape[1] for x in (near, far))
    anywhere = pl.BlockSpec(memory_space=pl.ANY)
    plane = near.shape[0]
    return pl.pallas_call(
        attend_kernel,
        grid_spec=pltpu.PrefetchScalarGridSpec(
            num_scalar_prefetch=1,
            grid=(LOCAL // PAIR,),
            in_specs=[
                pl.BlockSpec((PAIR * BLK, HEADS * DK), lambda b, src: (b, 0)),
                pl.BlockSpec((PAIR * BLK, HEADS * DV), lambda b, src: (b, 0)),
                anywhere,
                anywhere,
                anywhere,
            ],
            out_specs=[
                pl.BlockSpec((PAIR * BLK, HEADS * DV), lambda b, src: (b, 0)),
                pl.BlockSpec((PAIR * BLK, HEADS * DK), lambda b, src: (b, 0)),
                anywhere,
                anywhere,
                anywhere,
                pl.BlockSpec((LOCAL, ROWS, 128), lambda b, src: (0, 0, 0)),
            ],
            scratch_shapes=[
                pltpu.VMEM((n_near + n_far + LOCAL, ROWS, 128), BF),
                pltpu.VMEM((n_near + n_far + 1, ROWS, 128), BF),
                pltpu.VMEM((PAIR, keys, 256), BF),
                pltpu.VMEM((PAIR, keys, 256), BF),
                pltpu.VMEM((PAIR, 2, rows, 256), BF),
                pltpu.VMEM((PAIR, rows, 256), BF),
                pltpu.VMEM((PAIR, keys, rows), F32),
                pltpu.VMEM((PAIR, keys, rows), BF),
                pltpu.VMEM((PAIR, keys, 256), F32),
                pltpu.VMEM((PAIR, keys, 128), F32),
                pltpu.SemaphoreType.DMA((5,)),
            ],
        ),
        out_shape=(
            jax.ShapeDtypeStruct((tokens, HEADS * DV), BF),
            jax.ShapeDtypeStruct((tokens, HEADS * DK), BF),
            jax.ShapeDtypeStruct((plane, ROWS, 128), BF),
            jax.ShapeDtypeStruct((plane, 2, ROWS, 128), BF),
            jax.ShapeDtypeStruct((n_far, ROWS, 128), BF),
            jax.ShapeDtypeStruct((LOCAL, ROWS, 128), F32),
        ),
        compiler_params=params(),
        name="attend",
    )(
        src,
        queries,
        d_out,
        local,
        near,
        far.reshape(n_far, ROWS, 128),
    )


def pass_on(terms, perm):
    total = lax.ppermute(terms[0], "z", perm)
    for term in terms[1:]:
        total = (total.astype(F32) + term.astype(F32)).astype(BF)
        total = lax.ppermute(total, "z", perm)
    return total


def shards(depth, plane, queries, keys, values, selected, d_out):
    me = lax.axis_index(("z", "y", "x"))
    z = lax.axis_index("z")
    seq_count = depth * plane
    per_half = LOCAL // 2
    half_index = selected // per_half
    is_late = half_index >= seq_count
    owners = jnp.where(is_late, 2 * seq_count - 1 - half_index, half_index)
    inner = selected % per_half + jnp.where(is_late, per_half, 0)
    remote = owners != me
    offset = (owners // plane - z + depth) % depth
    order = jnp.where(offset < 2, offset, jnp.where(offset == depth - 1, 2, offset + 1))
    in_plane = owners % plane
    slots = jnp.where(
        order < 3, order * plane + in_plane, 3 * plane + in_plane * (depth - 3) + order - 3
    )
    src = jnp.where(remote, slots, seq_count + inner).astype(jnp.int32)
    flat = jnp.where(remote, in_plane * depth + order, -1).reshape(-1)
    hits = flat[:, None] == jnp.arange(seq_count, dtype=jnp.int32)[None, :]
    wanted = jnp.max(jnp.where(hits, inner.reshape(-1)[:, None] + 1, 0), axis=0)
    exchange = functools.partial(
        lax.all_to_all, axis_name=("y", "x"), split_axis=0, concat_axis=0, tiled=True
    )
    up = [(i, (i + 1) % depth) for i in range(depth)]
    down = [(i, (i - 1) % depth) for i in range(depth)]

    local = pack(keys.T, values)
    above, below = [local], [local]
    for _ in range(depth // 2):
        above.append(lax.ppermute(above[-1], "z", down))
    for _ in range(depth - 1 - depth // 2):
        below.append(lax.ppermute(below[-1], "z", up))
    asked = exchange(wanted.reshape(plane, 1, depth)).reshape(plane, depth)
    near = exchange(build(0, 16, asked, local, above[1], below[1]))
    far = exchange(build(3, 56, asked, *above[2:], *below[:1:-1]))
    attended, d_queries, part_here, part_side, part_far, own = attend(
        src, queries, d_out, local, near, far
    )
    far_sums = sum_returned(3, asked, exchange(part_far.reshape(far.shape)))
    *far_sums, part_side = lax.optimization_barrier((*far_sums, part_side))
    n_above = depth // 2 - 1
    to_above, to_below = far_sums[:n_above][::-1], far_sums[n_above:]
    side_above, side_below = sum_returned(1, asked, exchange(part_side))
    *sides, part_here = lax.optimization_barrier((side_above, side_below, part_here))
    rising = pass_on(to_above + sides[:1], up)
    falling = pass_on(to_below + sides[1:], down)
    d_keys_t, d_values = finish(asked, own, exchange(part_here[:, None]), rising, falling)
    return attended, d_queries, d_keys_t.T, d_values


def solution(mesh):
    grid = Mesh(mesh.devices.reshape(SIDES + (-1,)), ("z", "y", "x", "grp"))
    spec = P(("z", "y", "x"), "grp")
    return jax.shard_map(
        functools.partial(shards, SIDES[0], SIDES[1] * SIDES[2]),
        mesh=grid,
        in_specs=(spec,) * 5,
        out_specs=(spec,) * 4,
        check_vma=False,
    )
```

```python
import functools

import jax
import jax.numpy as jnp
from jax import lax
from jax.experimental import pallas as pl
from jax.experimental.pallas import tpu as pltpu
from jax.sharding import Mesh, PartitionSpec as P

BLK = 64
SEL = 16
HEADS = 8
DK = 192
DV = 128
ROWS = 160
SIDES = (8, 4, 4)
LOCAL = 8
LOG2E = 1.4426950408889634
NEG = -1e30
BF = jnp.bfloat16
F32 = jnp.float32


def params(mib=56):
    return pltpu.CompilerParams(vmem_limit_bytes=mib * 1024 * 1024)


def pack_kernel(k_ref, v_ref, out_ref):
    for b in range(0, LOCAL, 2):
        pair = jnp.transpose(k_ref[:, b * BLK : (b + 2) * BLK])
        for i in range(2):
            k = pair[i * BLK : (i + 1) * BLK]
            out_ref[b + i, 0:BLK] = v_ref[(b + i) * BLK : (b + i + 1) * BLK, :]
            out_ref[b + i, BLK : 2 * BLK] = k[:, :128]
            low = k[:, 128:]
            out_ref[b + i, 2 * BLK :] = jnp.concatenate([low[:32], low[32:]], axis=1)


def pack(keys_t, values):
    return pl.pallas_call(
        pack_kernel,
        out_shape=jax.ShapeDtypeStruct((LOCAL, ROWS, 128), BF),
        compiler_params=params(16),
        name="pack",
    )(keys_t, values)


def build_kernel(first, req_ref, *refs):
    tables, out_hbm = refs[: (len(refs) - 3) // 2], refs[(len(refs) - 3) // 2]
    held, (load_sems, sems) = refs[-2 - len(tables) : -2], refs[-2:]
    plane, count = out_hbm.shape[:2]
    loads = [
        pltpu.make_async_copy(t, h, load_sems.at[i]) for i, (t, h) in enumerate(zip(tables, held))
    ]
    for load in loads:
        load.start()
    sends = []
    for d in range(count):
        loads[d].wait()
        for c in range(plane):
            r = jnp.maximum(req_ref[c, first + d], 1) - 1
            sends.append(pltpu.make_async_copy(held[d].at[r], out_hbm.at[c, d], sems.at[c, d]))
            sends[-1].start()
    for send in sends:
        send.wait()


def build(first, mib, req, *tables):
    plane, count = req.shape[0], len(tables)
    anywhere = pl.BlockSpec(memory_space=pl.ANY)
    return pl.pallas_call(
        functools.partial(build_kernel, first),
        grid_spec=pltpu.PrefetchScalarGridSpec(
            num_scalar_prefetch=1,
            grid=(1,),
            in_specs=[anywhere] * len(tables),
            out_specs=anywhere,
            scratch_shapes=[pltpu.VMEM(t.shape, BF) for t in tables]
            + [pltpu.SemaphoreType.DMA((len(tables),)), pltpu.SemaphoreType.DMA((plane, count))],
        ),
        out_shape=jax.ShapeDtypeStruct((plane, count, ROWS, 128), BF),
        compiler_params=params(mib),
        name="build",
    )(req, *tables)


def sum_blocks(first, req_ref, ret_hbm, buf, acc, staged, in_sems, out_sems, target):
    plane, count = ret_hbm.shape[:2]
    loads = [
        pltpu.make_async_copy(ret_hbm.at[:, d], buf.at[d], in_sems.at[d]) for d in range(count)
    ]
    for load in loads:
        load.start()
    stores = []
    for d in range(count):
        loads[d].wait()
        acc[...] = jnp.zeros_like(acc)
        for c in range(plane):
            acc[req_ref[c, first + d]] += buf[d, c].astype(F32)
        staged[d] = acc[1:].astype(BF)
        stores.append(pltpu.make_async_copy(staged.at[d], target(d), out_sems.at[d]))
        stores[-1].start()
    return stores


def sum_kernel(first, req_ref, ret_hbm, *refs):
    outs, (buf, acc, staged, in_sems, out_sems) = refs[:-5], refs[-5:]
    for store in sum_blocks(
        first, req_ref, ret_hbm, buf, acc, staged, in_sems, out_sems, lambda d: outs[d]
    ):
        store.wait()


def sum_scratch(plane, count, depth):
    return [
        pltpu.VMEM((count, plane, ROWS, 128), BF),
        pltpu.VMEM((LOCAL + 1, ROWS, 128), F32),
        pltpu.VMEM((count + 1, LOCAL, ROWS, 128), BF),
        pltpu.SemaphoreType.DMA((count,)),
        pltpu.SemaphoreType.DMA((depth,)),
    ]


def sum_returned(first, req, returned):
    plane, count = returned.shape[:2]
    anywhere = pl.BlockSpec(memory_space=pl.ANY)
    return pl.pallas_call(
        functools.partial(sum_kernel, first),
        grid_spec=pltpu.PrefetchScalarGridSpec(
            num_scalar_prefetch=1,
            grid=(1,),
            in_specs=[anywhere],
            out_specs=[anywhere] * count,
            scratch_shapes=sum_scratch(plane, count, count),
        ),
        out_shape=[jax.ShapeDtypeStruct((LOCAL, ROWS, 128), BF)] * count,
        compiler_params=params(16),
        name="sum_returned",
    )(req, returned)


def finish_kernel(req_ref, own_ref, ret_ref, rising_ref, falling_ref, dk_ref, dv_ref, acc):
    acc[1:] = own_ref[...] + rising_ref[...].astype(F32) + falling_ref[...].astype(F32)
    for c in range(ret_ref.shape[0]):
        acc[req_ref[c, 0]] += ret_ref[c, 0].astype(F32)
    for b in range(0, LOCAL, 2):
        pair = []
        for i in range(b, b + 2):
            total = acc[i + 1]
            dv_ref[i * BLK : (i + 1) * BLK, :] = total[0:BLK].astype(BF)
            low = total[2 * BLK :]
            low = jnp.concatenate([low[:, :64], low[:, 64:]], axis=0)
            pair.append(jnp.concatenate([total[BLK : 2 * BLK], low], axis=1))
        pair = jnp.concatenate(pair, axis=0)
        dk_ref[:, b * BLK : (b + 2) * BLK] = jnp.transpose(pair).astype(BF)


def finish(req, own, returned, rising, falling):
    def whole(dims):
        return pl.BlockSpec(dims, lambda i, req: (0,) * len(dims))

    outs = ((DK, LOCAL * BLK), (LOCAL * BLK, DV))
    return pl.pallas_call(
        finish_kernel,
        grid_spec=pltpu.PrefetchScalarGridSpec(
            num_scalar_prefetch=1,
            grid=(1,),
            in_specs=[whole(x.shape) for x in (own, returned, rising, falling)],
            out_specs=[whole(dims) for dims in outs],
            scratch_shapes=[pltpu.VMEM((LOCAL + 1, ROWS, 128), F32)],
        ),
        out_shape=[jax.ShapeDtypeStruct(dims, BF) for dims in outs],
        compiler_params=params(16),
        name="finish",
    )(req, own, returned, rising, falling)


def dot(a, b, da, db):
    return lax.dot_general(a, b, (((da,), (db,)), ((), ())), preferred_element_type=F32)


def swap(x):
    return jnp.concatenate([x[:, 64:], x[:, :64]], axis=1)


HALF_BLK = BLK // 2
GROUP = SEL * HALF_BLK
PAIR = 4


def lane_ids(rows):
    return lax.broadcasted_iota(jnp.int32, (rows, 128), 1)


def attend_kernel(
    src_ref,
    q_ref,
    do_ref,
    local_hbm,
    near_hbm,
    far_hbm,
    att_ref,
    dq_ref,
    part_here_hbm,
    part_side_hbm,
    part_far_hbm,
    own_ref,
    table,
    part,
    k_bufs,
    v_bufs,
    q_bufs,
    do_bufs,
    p_bufs,
    pb_bufs,
    dk_bufs,
    dv_bufs,
    sems,
):
    step = pl.program_id(0)
    plane, n_far = near_hbm.shape[0], far_hbm.shape[0]
    n_near = plane * near_hbm.shape[1]
    n_remote = n_near + n_far
    scale = DK**-0.5
    left = lane_ids(HALF_BLK) < 64
    lane = lane_ids(BLK)
    first = lane < 64
    groups = [slice(0, GROUP), slice(GROUP, 2 * GROUP)]

    loads = [(near_hbm.at[:, d], d * plane, plane) for d in range(near_hbm.shape[1])]
    loads += [(local_hbm, n_remote, LOCAL), (far_hbm, n_near, n_far)]
    loads = [
        pltpu.make_async_copy(ref, table.at[pl.ds(at, n)], sems.at[i])
        for i, (ref, at, n) in enumerate(loads)
    ]
    stores = [(part_far_hbm, n_near, n_far), (part_here_hbm, 0, plane)]
    stores += [
        (part_side_hbm.at[:, d], (d + 1) * plane, plane) for d in range(part_side_hbm.shape[1])
    ]
    stores = [
        pltpu.make_async_copy(part.at[pl.ds(at, n)], ref, sems.at[i])
        for i, (ref, at, n) in enumerate(stores)
    ]

    @pl.when(step == 0)
    def _():
        for load in loads:
            load.start()
        own_ref[...] = jnp.zeros_like(own_ref)
        for i in range(PAIR):
            v_bufs[i, :, 128:] = jnp.ones((2 * GROUP, 128), BF)

    class Block:
        def __init__(self, i):
            self.i, self.b = i, step * PAIR + i
            self.rows = slice(i * BLK, (i + 1) * BLK)
            self.k, self.v, self.q, self.do = (x.at[i] for x in (k_bufs, v_bufs, q_bufs, do_bufs))
            self.p, self.pb, self.dk, self.dv = (x.at[i] for x in (p_bufs, pb_bufs, dk_bufs, dv_bufs))

        def place_keys(self):
            key_id = lax.broadcasted_iota(jnp.int32, (HALF_BLK, 128), 0)
            query_id = lane_ids(HALF_BLK) % BLK
            none = jnp.zeros((HALF_BLK, 128), BF)
            masks = [
                jnp.where(key_id + g * HALF_BLK > query_id, NEG, 0.0).astype(BF) for g in range(2)
            ]
            for e in range(SEL):
                s = src_ref[self.b, e]
                mine = s == n_remote + self.b
                low = table[s, 2 * BLK :]
                for g in range(2):
                    at = g * GROUP + e * HALF_BLK
                    rows = slice(at, at + HALF_BLK)
                    self.v[rows, 0:128] = table[s, g * HALF_BLK : (g + 1) * HALF_BLK]
                    self.k[rows, 0:128] = table[s, BLK + g * HALF_BLK : BLK + (g + 1) * HALF_BLK]
                    mask = jnp.where(mine, masks[g], none)
                    both = (low, mask) if g == 0 else (mask, low)
                    self.k[rows, 128:] = jnp.where(left, *both)

        def place_queries(self):
            one_hot = (lax.broadcasted_iota(jnp.int32, (BLK, 128), 0) == lane % BLK).astype(BF)
            for h in range(0, HEADS, 2):
                t0, t1, t2 = (
                    q_ref[self.rows, h * DK + i * 128 : h * DK + (i + 1) * 128] for i in range(3)
                )
                r1, r2 = swap(t1), swap(t2)
                for k, (high, low, swapped) in enumerate(
                    ((t0, t1, r1), (jnp.where(first, r1, r2), r2, t2))
                ):
                    rows = slice((h + k) * BLK, (h + k + 1) * BLK)
                    for g in range(2):
                        self.q[g, rows, 0:128] = high
                    self.q[0, rows, 128:] = jnp.where(first, low, one_hot)
                    self.q[1, rows, 128:] = jnp.where(first, one_hot, swapped)

        def score(self):
            self.top = None
            for g, rows in enumerate(groups):
                s = dot(self.k[rows, :], self.q[g], 1, 1)
                self.p[rows, :] = s
                m = jnp.max(s, axis=0, keepdims=True)
                self.top = m if self.top is None else jnp.maximum(self.top, m)

        def weigh(self):
            self.out_t = None
            for rows in groups:
                p = jnp.exp2((self.p[rows, :] - self.top) * (scale * LOG2E))
                self.p[rows, :] = p
                pb = p.astype(BF)
                self.pb[rows, :] = pb
                o = dot(self.v[rows, : DV + 16], pb, 0, 0)
                self.out_t = o if self.out_t is None else self.out_t + o

        def output(self):
            out = jnp.transpose(self.out_t)
            inverse = 1.0 / out[:, 128:129]
            att = (out[:, :128] * inverse).astype(BF)
            for h in range(HEADS):
                rows = slice(h * BLK, (h + 1) * BLK)
                cols = slice(h * DV, (h + 1) * DV)
                att_ref[self.rows, cols] = att[rows]
                do = (do_ref[self.rows, cols].astype(F32) * inverse[rows]).astype(BF)
                delta = jnp.sum(do.astype(F32) * att[rows].astype(F32), axis=1, keepdims=True)
                delta = jnp.broadcast_to(-delta, (BLK, 128))
                high = delta.astype(BF).astype(F32)
                rest = delta - high
                mid = rest.astype(BF).astype(F32)
                extra = jnp.where(
                    lane == 0, high, jnp.where(lane == 1, mid, jnp.where(lane == 2, rest - mid, 0.0))
                )
                self.do[rows, 0:128] = do
                self.do[rows, 128:] = extra.astype(BF)

        def backward(self):
            do_all = self.do[...]
            self.dq_t = []
            for g, rows in enumerate(groups):
                dp = dot(self.v[rows, :], do_all, 1, 1)
                ds = (self.p[rows, :] * dp).astype(BF)
                self.dv[rows, :] = dot(self.pb[rows, :], self.do[:, 0:128], 1, 0)
                self.dk[rows, :] = dot(ds, self.q[g], 1, 0) * scale
                self.dq_t.append(dot(self.k[rows, :], ds, 0, 0))

        def packed(self, e):
            r1 = slice(e * HALF_BLK, (e + 1) * HALF_BLK)
            r2 = slice(GROUP + e * HALF_BLK, GROUP + (e + 1) * HALF_BLK)
            return (
                (slice(0, HALF_BLK), self.dv[r1, :]),
                (slice(HALF_BLK, BLK), self.dv[r2, :]),
                (slice(BLK, BLK + HALF_BLK), self.dk[r1, 0:128]),
                (slice(BLK + HALF_BLK, 2 * BLK), self.dk[r2, 0:128]),
                (slice(2 * BLK, ROWS), jnp.where(left, self.dk[r1, 128:], self.dk[r2, 128:])),
            )

        def store_parts(self):
            for e in range(SEL):
                at = jnp.minimum(src_ref[self.b, e], n_remote)
                for rows, x in self.packed(e):
                    part[at, rows] = x.astype(BF)

        def add_own(self):
            for rows, x in self.packed(0):
                own_ref[self.b, rows] += x
            for e in range(1, SEL):
                s = src_ref[self.b, e]

                @pl.when(s >= n_remote)
                def _():
                    for rows, x in self.packed(e):
                        own_ref[s - n_remote, rows] += x

        def query_grads(self):
            high = jnp.transpose(self.dq_t[0][:128] + self.dq_t[1][:128]) * scale
            low = self.dq_t[0][128:192] + self.dq_t[1][192:]
            low = jnp.transpose(jnp.concatenate([low, low], axis=0)) * scale
            for h in range(0, HEADS, 2):
                even, odd = slice(h * BLK, (h + 1) * BLK), slice((h + 1) * BLK, (h + 2) * BLK)
                turned = swap(high[odd])
                parts = (
                    high[even],
                    jnp.where(first, low[even], turned),
                    jnp.where(first, turned, low[odd]),
                )
                for i, x in enumerate(parts):
                    dq_ref[self.rows, h * DK + i * 128 : h * DK + (i + 1) * 128] = x.astype(BF)

    blocks = [Block(i) for i in range(PAIR)]
    for block in blocks:
        block.place_queries()

    @pl.when(step == 0)
    def _():
        for load in loads:
            load.wait()

    blocks[0].place_keys()
    blocks[1].place_keys()
    blocks[0].score()
    blocks[2].place_keys()
    blocks[1].score()
    blocks[0].weigh()
    blocks[3].place_keys()
    blocks[2].score()
    blocks[1].weigh()
    blocks[0].output()
    blocks[3].score()
    blocks[2].weigh()
    blocks[1].output()
    blocks[0].backward()
    blocks[3].weigh()
    blocks[2].output()
    blocks[1].backward()
    blocks[0].store_parts()
    blocks[3].output()
    blocks[2].backward()
    blocks[1].store_parts()
    blocks[3].backward()
    blocks[2].store_parts()
    blocks[3].store_parts()
    last = step == LOCAL // PAIR - 1

    @pl.when(last)
    def _():
        for store in stores:
            store.start()

    for block in blocks:
        block.query_grads()
    for block in blocks:
        block.add_own()

    @pl.when(last)
    def _():
        for store in stores:
            store.wait()


def attend(src, queries, d_out, local, near, far):
    tokens = LOCAL * BLK
    keys = SEL * BLK
    rows = HEADS * BLK
    n_near, n_far = (x.shape[0] * x.shape[1] for x in (near, far))
    anywhere = pl.BlockSpec(memory_space=pl.ANY)
    plane = near.shape[0]
    return pl.pallas_call(
        attend_kernel,
        grid_spec=pltpu.PrefetchScalarGridSpec(
            num_scalar_prefetch=1,
            grid=(LOCAL // PAIR,),
            in_specs=[
                pl.BlockSpec((PAIR * BLK, HEADS * DK), lambda b, src: (b, 0)),
                pl.BlockSpec((PAIR * BLK, HEADS * DV), lambda b, src: (b, 0)),
                anywhere,
                anywhere,
                anywhere,
            ],
            out_specs=[
                pl.BlockSpec((PAIR * BLK, HEADS * DV), lambda b, src: (b, 0)),
                pl.BlockSpec((PAIR * BLK, HEADS * DK), lambda b, src: (b, 0)),
                anywhere,
                anywhere,
                anywhere,
                pl.BlockSpec((LOCAL, ROWS, 128), lambda b, src: (0, 0, 0)),
            ],
            scratch_shapes=[
                pltpu.VMEM((n_near + n_far + LOCAL, ROWS, 128), BF),
                pltpu.VMEM((n_near + n_far + 1, ROWS, 128), BF),
                pltpu.VMEM((PAIR, keys, 256), BF),
                pltpu.VMEM((PAIR, keys, 256), BF),
                pltpu.VMEM((PAIR, 2, rows, 256), BF),
                pltpu.VMEM((PAIR, rows, 256), BF),
                pltpu.VMEM((PAIR, keys, rows), F32),
                pltpu.VMEM((PAIR, keys, rows), BF),
                pltpu.VMEM((PAIR, keys, 256), F32),
                pltpu.VMEM((PAIR, keys, 128), F32),
                pltpu.SemaphoreType.DMA((5,)),
            ],
        ),
        out_shape=(
            jax.ShapeDtypeStruct((tokens, HEADS * DV), BF),
            jax.ShapeDtypeStruct((tokens, HEADS * DK), BF),
            jax.ShapeDtypeStruct((plane, ROWS, 128), BF),
            jax.ShapeDtypeStruct((plane, 2, ROWS, 128), BF),
            jax.ShapeDtypeStruct((n_far, ROWS, 128), BF),
            jax.ShapeDtypeStruct((LOCAL, ROWS, 128), F32),
        ),
        compiler_params=params(48),
        name="attend",
    )(
        src,
        queries,
        d_out,
        local,
        near,
        far.reshape(n_far, ROWS, 128),
    )


def pass_on(terms, perm):
    total = lax.ppermute(terms[0], "z", perm)
    for term in terms[1:]:
        total = (total.astype(F32) + term.astype(F32)).astype(BF)
        total = lax.ppermute(total, "z", perm)
    return total


def shards(depth, plane, queries, keys, values, selected, d_out):
    me = lax.axis_index(("z", "y", "x"))
    z = lax.axis_index("z")
    seq_count = depth * plane
    per_half = LOCAL // 2
    half_index = selected // per_half
    is_late = half_index >= seq_count
    owners = jnp.where(is_late, 2 * seq_count - 1 - half_index, half_index)
    inner = selected % per_half + jnp.where(is_late, per_half, 0)
    remote = owners != me
    offset = (owners // plane - z + depth) % depth
    order = jnp.where(offset < 2, offset, jnp.where(offset == depth - 1, 2, offset + 1))
    in_plane = owners % plane
    slots = jnp.where(
        order < 3, order * plane + in_plane, 3 * plane + in_plane * (depth - 3) + order - 3
    )
    src = jnp.where(remote, slots, seq_count + inner).astype(jnp.int32)
    flat = jnp.where(remote, in_plane * depth + order, -1).reshape(-1)
    hits = flat[:, None] == jnp.arange(seq_count, dtype=jnp.int32)[None, :]
    wanted = jnp.max(jnp.where(hits, inner.reshape(-1)[:, None] + 1, 0), axis=0)
    exchange = functools.partial(
        lax.all_to_all, axis_name=("y", "x"), split_axis=0, concat_axis=0, tiled=True
    )
    up = [(i, (i + 1) % depth) for i in range(depth)]
    down = [(i, (i - 1) % depth) for i in range(depth)]

    local = pack(keys.T, values)
    above, below = [local], [local]
    for _ in range(depth // 2):
        above.append(lax.ppermute(above[-1], "z", down))
    for _ in range(depth - 1 - depth // 2):
        below.append(lax.ppermute(below[-1], "z", up))
    asked = exchange(wanted.reshape(plane, 1, depth)).reshape(plane, depth)
    near = exchange(build(0, 16, asked, local, above[1], below[1]))
    far = exchange(build(3, 56, asked, *above[2:], *below[:1:-1]))
    attended, d_queries, part_here, part_side, part_far, own = attend(
        src, queries, d_out, local, near, far
    )
    far_sums = sum_returned(3, asked, exchange(part_far.reshape(far.shape)))
    *far_sums, part_side = lax.optimization_barrier((*far_sums, part_side))
    n_above = depth // 2 - 1
    to_above, to_below = far_sums[:n_above][::-1], far_sums[n_above:]
    side_above, side_below = sum_returned(1, asked, exchange(part_side))
    *sides, part_here = lax.optimization_barrier((side_above, side_below, part_here))
    rising = pass_on(to_above + sides[:1], up)
    falling = pass_on(to_below + sides[1:], down)
    d_keys_t, d_values = finish(asked, own, exchange(part_here[:, None]), rising, falling)
    return attended, d_queries, d_keys_t.T, d_values


def solution(mesh):
    grid = Mesh(mesh.devices.reshape(SIDES + (-1,)), ("z", "y", "x", "grp"))
    spec = P(("z", "y", "x"), "grp")
    return jax.shard_map(
        functools.partial(shards, SIDES[0], SIDES[1] * SIDES[2]),
        mesh=grid,
        in_specs=(spec,) * 5,
        out_specs=(spec,) * 4,
        check_vma=False,
    )
```
